768 devices in a mesh: dp: 12 (over z), seq: 8 (over x, core), head: 8 (over y).
Axes of the slice: x: 4, y: 8, z: 12, core: 2. Of those that a mesh axis runs over, the one named last changes fastest.
Arguments:
- tokens: bfloat16 [98304, 1536], P(('dp', 'seq', 'head')), may hold values from -6 to 6
- norm_gain: float32 [1536], replicated, may hold values from 0.5 to 1.5
- w_up: bfloat16 [64, 1536, 1536], P(('seq', 'head')), may hold values from -0.15625 to 0.15625
- w_down: bfloat16 [64, 1536, 1536], P(('seq', 'head')), may hold values from -0.15625 to 0.15625
- routes: int32 [98304, 2], P(('dp', 'seq', 'head')), may hold values from 0 to 63, all different within a row; in each aligned block of 128 rows (0 to 127, 128 to 255, ...) at most 4 rows name the same one
- combine: float32 [98304, 2], P(('dp', 'seq', 'head')), may hold values from 0.1 to 1
- loss_mask: int32 [98304], P(('dp', 'seq', 'head')), may hold values from 0 to 1, as said below
Outputs:
- grad_tokens: bfloat16 [98304, 1536], P(('dp', 'seq', 'head'))
- grad_gain: float32 [1536], replicated
- grad_combine: float32 [98304, 2], P(('dp', 'seq', 'head'))
- loss_value: float32 [], replicated
The draws below stay inside these ranges and needn't reach their ends.
Inputs may be any that keep to these rules, and one draw needn't show every extreme that they name: `routes`: the 2 experts of a token differ. Among the tokens of one device no expert is named more than 4 times; every expert is named somewhere. `loss_mask`: every eighth token (positions 7, 15, 23, ...) has 1.
All inputs are finite; a program needn't handle non-finite values.
Results may differ from the reference program's by a relative error of at most 0.0085.
Values may be sent and summed in bfloat16 or wider, within the bound.
A program may use at most 64 MiB of HBM per device.

```python
import math
import jax
import jax.numpy as jnp
import numpy as np
from jax import lax

D = 1536
FF = 1536
TOP = 2
TOK_DEV = 128
EXPERTS = 64
CAP = 4
TOKENS = 98304


def draw_loss_mask(key, part):
    key = jax.random.fold_in(key, 11)
    rate_key = jax.random.fold_in(key, 1)
    pick_key = jax.random.fold_in(key, 2)
    factor = jax.random.randint(rate_key, (), 200, 1001, dtype=jnp.int32)
    position = jnp.arange(TOKENS, dtype=jnp.int32)
    base = 250 + 500 * position // TOKENS
    limit = factor * base // 1000
    limit = jnp.where(position % 8 == 7, 1000, limit)
    picks = jax.random.randint(pick_key, (TOKENS,), 0, 1000, dtype=jnp.int32)
    return (picks < limit).astype(jnp.int32)


def levels(stream_key, shape, shards, smallest, high):
    level = 1.0
    for dim, blocks in shards:
        heights = jax.random.uniform(jax.random.fold_in(jax.random.fold_in(stream_key, 6), dim), (blocks,), jnp.float32, smallest / len(shards), high / len(shards))
        level = level * jnp.repeat(jnp.exp(heights), shape[dim] // blocks).reshape((-1,) + (1,) * (len(shape) - 1 - dim))
    return level


def routed_block(stream_key, own, number, rows, count, top, reach, skew):
    order = jax.random.permutation(stream_key, count)
    crowded, common = shares(count, rows * top, reach, skew, True), shares(count, rows * top, reach, skew, False)
    places = jnp.arange(count)

    def named(sizes, rotation):
        used = int((sizes > 0).sum())
        fixed = max(1, used // 4)
        shifted = fixed + (places - fixed + rotation * (used - fixed)) % max(1, count - fixed)
        return jnp.zeros((count,), jnp.int32).at[order[jnp.where(places < fixed, places, shifted)]].set(jnp.asarray(sizes, jnp.int32))

    sizes = jnp.where(number % 4 == 0, named(crowded, number // 4), named(common, number - number // 4 - 1))
    mixed = jax.random.permutation(jax.random.fold_in(own, 3), count)
    donor, sink = mixed[0:count // 2 * 2:2], mixed[1:count // 2 * 2:2]
    room = jnp.minimum(sizes[donor] - 1, reach - sizes[sink]) // 2
    room = jnp.where((donor == order[0]) | (sink == order[0]) | (sizes[sink] == 0), 0, jnp.maximum(room, 0))
    shifted = jax.random.randint(jax.random.fold_in(own, 4), (count // 2,), 0, 1 << 20) % (room + 1)
    sizes = sizes.at[donor].add(-shifted).at[sink].add(shifted)
    items = jnp.searchsorted(jnp.cumsum(sizes), jnp.arange(rows * top), side="right").astype(jnp.int32)
    table = items.reshape(top, rows).T
    table = table[jax.random.permutation(jax.random.fold_in(own, 1), rows)]
    rotation = jax.random.randint(jax.random.fold_in(own, 2), (rows, 1), 0, top)
    return jnp.take_along_axis(table, (jnp.arange(top)[None, :] + rotation) % top, axis=1)


def shares(amount, total, reach, lean, full):
    loads = [(1 << 20) // math.isqrt(rank ** lean) + 1 for rank in range(1, amount + 1)]
    largest = reach if full else min(reach, max(-(-total // amount), total * loads[0] // sum(loads)))
    least = 1 if total - largest >= amount - 1 else 0
    given, surplus = [largest] + [least] * (amount - 1), total - largest - least * (amount - 1)
    while surplus > 0:
        candidates = [i for i in range(1, amount) if given[i] < largest] or [i for i in range(1, amount) if given[i] < reach]
        pool, left = sum([loads[i] for i in candidates]), surplus
        for i in candidates:
            extra = min(reach - given[i], max(1, left * loads[i] // pool), surplus)
            given[i] = given[i] + extra
            surplus = surplus - extra
    return np.array(given)


def scatter_about(stream_key, shape, scale, most, split=(), kind=jnp.bfloat16):
    array = scale * jax.random.normal(stream_key, shape, jnp.float32)
    if split:
        array = array * levels(stream_key, shape, split, -0.22, 0.18)
    return jnp.clip(array, -most, most).astype(kind)


def setup_inputs(seed: int = 0) -> dict:
    seeds = jax.random.split(jax.random.key(seed), 8)
    tokens = scatter_about(seeds[0], (TOKENS, D), 1.0, 6.0, ((0, 768),))
    norm_gain = jnp.clip(1.0 + 0.1 * jax.random.normal(seeds[1], (D,), jnp.float32), 0.5, 1.5)
    w_up = scatter_about(seeds[2], (EXPERTS, D, FF), D ** -0.5, 0.15625, ((0, 64),))
    w_down = scatter_about(seeds[3], (EXPERTS, FF, D), FF ** -0.5, 0.15625, ((0, 64),))
    routes_keys = jax.random.split(jax.random.fold_in(seeds[4], 1), TOKENS // TOK_DEV)
    routes_turns = jax.random.permutation(jax.random.fold_in(seeds[4], 3), TOKENS // TOK_DEV)
    routes = jax.vmap(lambda own, number: routed_block(jax.random.fold_in(seeds[4], 2), own, number, TOK_DEV, EXPERTS, TOP, CAP, 0))(routes_keys, routes_turns).reshape((TOKENS, TOP))
    combine = jnp.clip(0.1 + 0.9 * jax.random.uniform(seeds[5], (TOKENS, TOP), jnp.float32) ** levels(seeds[5], (TOKENS, TOP), ((0, 768),), -0.2, 0.2), 0.1, 1.0)
    loss_mask = draw_loss_mask(jax.random.fold_in(seeds[7], 71), 0)
    return {"tokens": tokens, "norm_gain": norm_gain, "w_up": w_up, "w_down": w_down, "routes": routes, "combine": combine, "loss_mask": loss_mask}


def reference(tokens, norm_gain, w_up, w_down, routes, combine, loss_mask):
    dev_count = TOKENS // TOK_DEV
    per_dev = TOK_DEV * TOP
    inputs = tokens.astype(jnp.float32)
    inverse = lax.rsqrt(lax.optimization_barrier(jnp.mean(inputs * inputs, axis=-1, keepdims=True)) + 1e-05)
    normed = inputs * inverse
    scaled = (normed * norm_gain).astype(jnp.bfloat16)
    flat_routes = routes.reshape(dev_count, per_dev).astype(jnp.int32)
    onehot = (flat_routes[:, :, None] == jnp.arange(EXPERTS, dtype=jnp.int32)[None, None, :]).astype(jnp.int32)
    position = lax.optimization_barrier(jnp.sum((jnp.cumsum(onehot, axis=1) - onehot) * onehot, axis=-1)).astype(jnp.int32)
    source = jnp.broadcast_to(jnp.arange(dev_count, dtype=jnp.int32)[:, None], (dev_count, per_dev))
    slot_ids = jnp.arange(TOKENS * TOP, dtype=jnp.int32).reshape(dev_count, per_dev)
    table = jnp.full((EXPERTS, dev_count, CAP), TOKENS * TOP, jnp.int32)
    table = table.at[flat_routes, source, position].set(slot_ids).reshape(EXPERTS, dev_count * CAP)
    padded_in = jnp.concatenate([scaled, jnp.zeros((1, D), jnp.bfloat16)], axis=0)

    def expert_forward(operands):
        chosen, weight_up, weight_down = operands
        gathered = padded_in[chosen // TOP]
        projected = jnp.dot(gathered, weight_up, preferred_element_type=jnp.float32)
        gate_value = jax.nn.sigmoid(1.702 * projected)
        hidden = (projected * gate_value).astype(jnp.bfloat16)
        result = jnp.dot(hidden, weight_down, preferred_element_type=jnp.float32).astype(jnp.bfloat16)
        return (result, projected)
    outputs, projections = lax.map(expert_forward, (table, w_up, w_down))
    flat_table = table.reshape(-1)
    slot_out = jnp.zeros((TOKENS * TOP + 1, D), jnp.bfloat16).at[flat_table].set(outputs.reshape(-1, D))
    slot_out = slot_out[:-1].reshape(TOKENS, TOP, D)
    mixed = inputs
    for slot_index in range(TOP):
        mixed = mixed + combine[:, slot_index, None] * slot_out[:, slot_index].astype(jnp.float32)
    mask_f = loss_mask.astype(jnp.float32)
    count = jnp.sum(mask_f)
    loss_value = jnp.sum(mask_f * lax.optimization_barrier(jnp.sum(mixed * mixed, axis=-1))) / (2.0 * D * count)
    cotangent = mask_f[:, None] * mixed
    ratio = TOKENS / count
    combine_terms = []
    cot_terms = []
    for slot_index in range(TOP):
        combine_terms.append(lax.optimization_barrier(jnp.sum(cotangent * slot_out[:, slot_index].astype(jnp.float32), axis=-1)))
        cot_terms.append((combine[:, slot_index, None] * cotangent).astype(jnp.bfloat16))
    grad_combine = ratio * jnp.stack(combine_terms, axis=1)
    scaled_cot = jnp.stack(cot_terms, axis=1).reshape(TOKENS * TOP, D)
    padded_cot = jnp.concatenate([scaled_cot, jnp.zeros((1, D), jnp.bfloat16)], axis=0)

    def expert_backward(operands):
        chosen, projected, weight_up, weight_down = operands
        incoming = padded_cot[chosen]
        hidden_grad = lax.dot_general(incoming, weight_down, (((1,), (1,)), ((), ())), preferred_element_type=jnp.float32)
        gate_value = jax.nn.sigmoid(1.702 * projected)
        slope = gate_value + 1.702 * projected * gate_value * (1.0 - gate_value)
        pre_grad = (hidden_grad * slope).astype(jnp.bfloat16)
        return lax.dot_general(pre_grad, weight_up, (((1,), (1,)), ((), ())), preferred_element_type=jnp.float32).astype(jnp.bfloat16)
    row_grads = lax.map(expert_backward, (table, projections, w_up, w_down))
    slot_grad = jnp.zeros((TOKENS * TOP + 1, D), jnp.bfloat16).at[flat_table].set(row_grads.reshape(-1, D))
    slot_grad = slot_grad[:-1].reshape(TOKENS, TOP, D)
    normed_total = jnp.zeros((TOKENS, D), jnp.float32)
    for slot_index in range(TOP):
        normed_total = normed_total + slot_grad[:, slot_index].astype(jnp.float32)
    grad_gain = lax.optimization_barrier(jnp.sum(normed_total * normed, axis=0)) / count
    normed_grad = normed_total * norm_gain
    input_grad = inverse * (normed_grad - normed * lax.optimization_barrier(jnp.mean(normed_grad * normed, axis=-1, keepdims=True)))
    grad_tokens = (ratio * (cotangent + input_grad)).astype(jnp.bfloat16)
    return (grad_tokens, grad_gain, grad_combine, loss_value)
```

```python
import jax
import jax.numpy as jnp
from jax import lax
from jax.experimental import pallas as pl
from jax.experimental.pallas import tpu as pltpu
from jax.sharding import PartitionSpec as P

F32, BF16, I32 = jnp.float32, jnp.bfloat16, jnp.int32
MESH = pl.DeviceIdType.MESH
CAP = 4
FOLD = 4
CHUNKS = 4
NT = (((1,), (1,)), ((), ()))


def dot(a, b):
    return jnp.dot(a, b, preferred_element_type=F32)


def iota(shape, dim):
    return lax.broadcasted_iota(I32, shape, dim)


def kernel(sizes, tok, gain, wup_hbm, wdown_hbm, routes, comb, mask,
           out_tok, out_gain, out_comb, out_loss,
           wup, wdown, snd, rcv, xs, slope, nat, sel, cot, stats, arz, ars, ary,
           send_sem, recv_sem, w_sem, red_send, red_recv):
    dp_n, seq_n, head_n = sizes
    rows, width = tok.shape
    peers = seq_n * head_n
    per = peers // CHUNKS
    msg = CAP * FOLD
    crow = per * msg
    cnat = per * CAP
    cols = width // FOLD
    slots = peers * CAP
    xn = seq_n // 2
    me_z = lax.axis_index("dp")
    me_s = lax.axis_index("seq")
    me_h = lax.axis_index("head")
    me_x, me_c = me_s // 2, me_s % 2

    def at_offset(g, i, sign):
        dc, dh = i % 2, i // 2
        dx = (g + dh) % xn
        x = (me_x + sign * dx + xn) % xn
        return {"seq": x * 2 + (me_c + dc) % 2, "head": (me_h + sign * dh + head_n) % head_n}

    load_up = pltpu.make_async_copy(wup_hbm.at[0], wup, w_sem.at[0])
    load_down = pltpu.make_async_copy(wdown_hbm.at[0], wdown, w_sem.at[1])
    load_up.start()
    load_down.start()

    barrier = pltpu.get_barrier_semaphore()

    def greet(j, _):
        pl.semaphore_signal(barrier, inc=1, device_id=at_offset(j // per, j % per, 1),
                            device_id_type=MESH)
        return _
    lax.fori_loop(1, peers, greet, 0)

    def greet_z(j, _):
        pl.semaphore_signal(barrier, inc=1, device_id={"dp": (me_z + j) % dp_n},
                            device_id_type=MESH)
        return _
    lax.fori_loop(1, dp_n, greet_z, 0)

    q, m = iota((crow, crow), 0), iota((crow, crow), 1)
    fold_m = (m == ((q // CAP) % FOLD) * cnat + (q // msg) * CAP + q % CAP).astype(BF16)
    back_m = (q == ((m // CAP) % FOLD) * cnat + (m // msg) * CAP + m % CAP).astype(BF16)

    def fold(block):
        stack = jnp.concatenate([block[:, c * cols:(c + 1) * cols] for c in range(FOLD)], axis=0)
        return dot(fold_m, stack).astype(BF16)

    def unfold(block):
        stack = dot(back_m, block).astype(BF16)
        return jnp.concatenate([stack[c * cnat:(c + 1) * cnat] for c in range(FOLD)], axis=1)

    def at(g, n):
        return pl.ds(pl.multiple_of(g * n, n), n)

    def start(phase, g, sign):
        def one(i, _):
            where = at(g * per + i, msg)
            pltpu.make_async_remote_copy(
                src_ref=snd.at[phase, where], dst_ref=rcv.at[phase, where],
                send_sem=send_sem.at[phase], recv_sem=recv_sem.at[phase, g],
                device_id=at_offset(g, i, sign), device_id_type=MESH).start()
            return _
        lax.fori_loop(1 if g == 0 else 0, per, one, 0)
        if g == 0:
            pltpu.make_async_copy(snd.at[phase, pl.ds(0, msg)], rcv.at[phase, pl.ds(0, msg)],
                                  recv_sem.at[phase, 0]).start()

    def arrived(phase, g):
        where = rcv.at[phase, at(g, crow)]
        pltpu.make_async_copy(where, where, recv_sem.at[phase, g]).wait()

    BR = 16

    def norm(b, _):
        r = at(b, BR)
        x = tok[r, :].astype(F32)
        inverse = lax.rsqrt(jnp.mean(x * x, axis=1, keepdims=True) + 1e-05)
        nat[r, :] = (x * inverse * gain[...]).astype(BF16)
        return _
    lax.fori_loop(0, rows // BR, norm, 0)

    eye = iota((rows, rows), 0) == iota((rows, rows), 1)
    lower = (iota((rows, rows), 0) > iota((rows, rows), 1)).astype(BF16)
    r0, r1 = routes[:, 0:1], routes[:, 1:2]
    lanes = iota((rows, peers), 1)
    hot0, hot1 = (lanes == r0).astype(F32), (lanes == r1).astype(F32)
    before = dot(lower, (hot0 + hot1).astype(BF16))

    def slot_of(r, hot):
        turn = jnp.sum(before * hot, axis=1, keepdims=True).astype(I32)
        s, h = r // head_n, r % head_n
        dx = (s // 2 - me_x + xn) % xn
        dc = (s % 2 + me_c) % 2
        dh = (h - me_h + head_n) % head_n
        g = (dx - dh + head_n) % xn
        return (g * per + dh * 2 + dc) * CAP + turn

    s0, s1 = slot_of(r0, hot0), slot_of(r1, hot1)

    def row_of(col):
        return jnp.sum(jnp.where(eye, col.astype(F32), 0.0), axis=0, keepdims=True)

    s0_row, s1_row = row_of(s0).astype(I32), row_of(s1).astype(I32)
    mask_col = jnp.sum(jnp.where(eye, mask[...].astype(F32), 0.0), axis=1, keepdims=True)
    slot_lanes = iota((rows, slots), 1)
    pick0 = (slot_lanes == s0).astype(BF16)
    pick1 = (slot_lanes == s1).astype(BF16)
    sel[0:rows, :] = pick0
    sel[rows:2 * rows, :] = pick1

    def place(g):
        target = iota((cnat, rows), 0) + g * cnat
        return (target == s0_row).astype(BF16), (target == s1_row).astype(BF16)

    for g in range(CHUNKS):
        a, b = place(g)
        block = dot(a + b, nat[0:rows, :]).astype(BF16)
        snd[0, g * crow:(g + 1) * crow, :] = fold(block)
        if g == 0:
            pl.semaphore_wait(barrier, peers - 1 + dp_n - 1)
        start(0, g, 1)

    load_up.wait()
    load_down.wait()
    tile = 512
    tiles = width // tile

    for g in range(CHUNKS):
        arrived(0, g)
        r = slice(g * cnat, (g + 1) * cnat)
        xs[r, :] = unfold(rcv[0, g * crow:(g + 1) * crow, :])

        def up(n, _):
            c = at(n, tile)
            projected = dot(xs[r, :], wup[:, c])
            gate = jax.nn.sigmoid(1.702 * projected)
            slope[r, c] = gate + 1.702 * projected * gate * (1.0 - gate)
            nat[0:cnat, c] = (projected * gate).astype(BF16)
            return _
        lax.fori_loop(0, tiles, up, 0)

        def down(n, _):
            c = at(n, tile)
            nat[cnat:2 * cnat, c] = dot(nat[0:cnat, :], wdown[:, c]).astype(BF16)
            return _
        lax.fori_loop(0, tiles, down, 0)
        snd[1, g * crow:(g + 1) * crow, :] = fold(nat[cnat:2 * cnat, :])
        start(1, g, -1)

    for g in range(CHUNKS):
        arrived(1, g)
        nat[g * cnat:(g + 1) * cnat, :] = unfold(rcv[1, g * crow:(g + 1) * crow, :])

    c0, c1 = comb[:, 0:1], comb[:, 1:2]

    loss = jnp.zeros((rows, 1), F32)
    part0 = jnp.zeros((rows, 1), F32)
    part1 = jnp.zeros((rows, 1), F32)
    for n in range(tiles):
        c = slice(n * tile, (n + 1) * tile)
        both = dot(sel[...], nat[:, c])
        p0, p1 = both[0:rows], both[rows:2 * rows]
        mixed = tok[:, c].astype(F32) + c0 * p0 + c1 * p1
        cotangent = mask_col * mixed
        cot[:, c] = cotangent
        loss = loss + jnp.sum(cotangent * mixed, axis=1, keepdims=True)
        part0 = part0 + jnp.sum(cotangent * p0, axis=1, keepdims=True)
        part1 = part1 + jnp.sum(cotangent * p1, axis=1, keepdims=True)
        nat[0:rows, c] = (c0 * cotangent).astype(BF16)
        nat[rows:2 * rows, c] = (c1 * cotangent).astype(BF16)

    for g in range(CHUNKS):
        a, b = place(g)
        block = dot(jnp.concatenate([a, b], axis=1), nat[...]).astype(BF16)
        snd[2, g * crow:(g + 1) * crow, :] = fold(block)
        start(2, g, 1)

    stats[...] = jnp.zeros_like(stats)
    stats[12:13, :] = jnp.broadcast_to(jnp.sum(loss, axis=0, keepdims=True), (1, 128))
    stats[13:14, :] = jnp.broadcast_to(jnp.sum(mask_col, axis=0, keepdims=True), (1, 128))

    gain_part = [jnp.zeros((1, tile), F32) for _ in range(tiles)]
    for g in range(CHUNKS):
        arrived(2, g)
        r = slice(g * cnat, (g + 1) * cnat)
        nat[0:cnat, :] = unfold(rcv[2, g * crow:(g + 1) * crow, :])

        def down_t(n, _):
            c = at(n, tile)
            hidden_grad = lax.dot_general(nat[0:cnat, :], wdown[c, :], NT,
                                          preferred_element_type=F32)
            nat[cnat:2 * cnat, c] = (hidden_grad * slope[r, c]).astype(BF16)
            return _
        lax.fori_loop(0, tiles, down_t, 0)
        for n in range(tiles):
            c = slice(n * tile, (n + 1) * tile)
            row_grad = lax.dot_general(nat[cnat:2 * cnat, :], wup[c, :], NT,
                                       preferred_element_type=F32).astype(BF16)
            gain_part[n] = gain_part[n] + jnp.sum(
                row_grad.astype(F32) * xs[r, c].astype(F32), axis=0, keepdims=True)
            nat[2 * cnat:3 * cnat, c] = row_grad
        snd[3, g * crow:(g + 1) * crow, :] = fold(nat[2 * cnat:3 * cnat, :])
        if g == CHUNKS - 1:
            for n in range(tiles):
                for k in range(tile // 128):
                    at_k = n * (tile // 128) + k
                    stats[at_k:at_k + 1, :] = (
                        gain_part[n][:, k * 128:(k + 1) * 128]
                        / gain[:, at_k * 128:(at_k + 1) * 128])
            reduce_start(0, dp_n, me_z, "dp", stats, arz, red_send, red_recv)
        start(3, g, -1)

    total = reduce_end(0, dp_n, arz, stats, red_send, red_recv)
    stats[...] = total
    reduce_start(1, seq_n, me_s, "seq", stats, ars, red_send, red_recv)
    total = reduce_end(1, seq_n, ars, stats, red_send, red_recv)
    stats[...] = total
    reduce_start(2, head_n, me_h, "head", stats, ary, red_send, red_recv)
    total = reduce_end(2, head_n, ary, stats, red_send, red_recv)
    stats[...] = total

    count = stats[13:14, 0:1]
    ratio = (rows * dp_n * peers) / count
    for k in range(width // 128):
        out_gain[:, k * 128:(k + 1) * 128] = stats[k:k + 1, :] / count
    out_loss[...] = stats[12:13, 0:1] / (2.0 * width * count)
    out_comb[:, 0:1] = ratio * part0
    out_comb[:, 1:2] = ratio * part1

    for g in range(CHUNKS):
        arrived(3, g)
        nat[g * cnat:(g + 1) * cnat, :] = unfold(rcv[3, g * crow:(g + 1) * crow, :])
    sel[0:rows, :] = sel[0:rows, :] + sel[rows:2 * rows, :]
    for n in range(tiles):
        c = slice(n * tile, (n + 1) * tile)
        slope[0:rows, c] = dot(sel[0:rows, :], nat[:, c])

    def last(b, _):
        r = at(b, BR)
        x = tok[r, :].astype(F32)
        inverse = lax.rsqrt(jnp.mean(x * x, axis=1, keepdims=True) + 1e-05)
        normed = x * inverse
        grad = slope[r, :] * gain[...]
        mean = jnp.mean(grad * normed, axis=1, keepdims=True)
        out_tok[r, :] = (ratio * (cot[r, :] + inverse * (grad - normed * mean))).astype(BF16)
        return _
    lax.fori_loop(0, rows // BR, last, 0)

    for phase in range(4):
        sent = snd.at[phase, pl.ds(msg, (peers - 1) * msg)]
        pltpu.make_async_copy(sent, sent, send_sem.at[phase]).wait()


def reduce_start(stage, n, me, axis, stats, parts, send_sem, recv_sem):
    parts[pl.ds(n, 1)] = stats[...][None]
    parts[pl.ds(me, 1)] = stats[...][None]

    def one(j, _):
        pltpu.make_async_remote_copy(
            src_ref=parts.at[pl.ds(n, 1)], dst_ref=parts.at[pl.ds(me, 1)],
            send_sem=send_sem.at[stage], recv_sem=recv_sem.at[stage],
            device_id={axis: (me + j) % n}, device_id_type=MESH).start()
        return _
    lax.fori_loop(1, n, one, 0)


def reduce_end(stage, n, parts, stats, send_sem, recv_sem):
    where = parts.at[pl.ds(0, n - 1)]
    pltpu.make_async_copy(where, where, recv_sem.at[stage]).wait()
    pltpu.make_async_copy(where, where, send_sem.at[stage]).wait()
    total = parts[0]
    for k in range(1, n):
        total = total + parts[k]
    return total


def solution(mesh):
    sizes = (mesh.shape["dp"], mesh.shape["seq"], mesh.shape["head"])

    def on_device(tokens, norm_gain, w_up, w_down, routes, combine, loss_mask):
        rows, width = tokens.shape
        peers = sizes[1] * sizes[2]
        slots = peers * CAP
        folded = (4, slots * FOLD, width // FOLD)
        vmem = pl.BlockSpec(memory_space=pltpu.VMEM)
        hbm = pl.BlockSpec(memory_space=pl.ANY)
        grad_tokens, grad_gain, grad_combine, loss = pl.pallas_call(
            lambda *refs: kernel(sizes, *refs),
            out_shape=(
                jax.ShapeDtypeStruct((rows, width), BF16),
                jax.ShapeDtypeStruct((1, width), F32),
                jax.ShapeDtypeStruct((rows, 2), F32),
                jax.ShapeDtypeStruct((1, 1), F32),
            ),
            in_specs=[vmem, vmem, hbm, hbm, vmem, vmem, vmem],
            out_specs=(vmem, vmem, vmem, vmem),
            scratch_shapes=[
                pltpu.VMEM(w_up.shape[1:], BF16),
                pltpu.VMEM(w_down.shape[1:], BF16),
                pltpu.VMEM(folded, BF16),
                pltpu.VMEM(folded, BF16),
                pltpu.VMEM((slots, width), BF16),
                pltpu.VMEM((slots, width), F32),
                pltpu.VMEM((slots, width), BF16),
                pltpu.VMEM((2 * rows, slots), BF16),
                pltpu.VMEM((rows, width), F32),
                pltpu.VMEM((16, 128), F32),
                pltpu.VMEM((sizes[0] + 1, 16, 128), F32),
                pltpu.VMEM((sizes[1] + 1, 16, 128), F32),
                pltpu.VMEM((sizes[2] + 1, 16, 128), F32),
                pltpu.SemaphoreType.DMA((4,)),
                pltpu.SemaphoreType.DMA((4, CHUNKS)),
                pltpu.SemaphoreType.DMA((2,)),
                pltpu.SemaphoreType.DMA((3,)),
                pltpu.SemaphoreType.DMA((3,)),
            ],
            compiler_params=pltpu.CompilerParams(
                collective_id=1, has_side_effects=True, vmem_limit_bytes=48 * 2**20),
            cost_estimate=pl.CostEstimate(
                flops=8 * slots * width * width, bytes_accessed=4 * width * width,
                transcendentals=slots * width),
            name="moe",
        )(tokens, norm_gain.reshape(1, width), w_up, w_down, routes, combine,
          loss_mask.reshape(1, rows))
        return grad_tokens, grad_gain.reshape(width), grad_combine, loss.reshape(())

    split = ("dp", "seq", "head")
    in_specs = (P(split, None), P(), P(("seq", "head"), None, None), P(("seq", "head"), None, None),
                P(split, None), P(split, None), P(split))
    out_specs = (P(split, None), P(), P(split, None), P())
    return jax.shard_map(on_device, mesh=mesh, in_specs=in_specs, out_specs=out_specs,
                         check_vma=False)
```

```python
import jax
import jax.numpy as jnp
from jax import lax
from jax.experimental import pallas as pl
from jax.experimental.pallas import tpu as pltpu
from jax.sharding import PartitionSpec as P

F32, BF16, I32 = jnp.float32, jnp.bfloat16, jnp.int32
MESH = pl.DeviceIdType.MESH
CAP = 4
FOLD = 4
CHUNKS = 4
NT = (((1,), (1,)), ((), ()))


def dot(a, b):
    return jnp.dot(a, b, preferred_element_type=F32)


def iota(shape, dim):
    return lax.broadcasted_iota(I32, shape, dim)


def kernel(sizes, tok_hbm, gain_hbm, wup_hbm, wdown_hbm, routes_hbm, comb_hbm, mask_hbm,
           out_tok, out_gain, out_comb, out_loss,
           tok, gain_v, routes, comb, mask, gain, inv,
           wup, wdown, snd, rcv, xs, slope, nat, sel, cot, stats, arz, ars, ary, num, cz, cs, cy,
           stats_all, num_all,
           send_sem, recv_sem, w_sem, red_send, red_recv, go, mate_send, mate_recv):
    dp_n, seq_n, head_n = sizes
    rows, width = tok.shape
    peers = seq_n * head_n
    per = peers // CHUNKS
    msg = CAP * FOLD
    crow = per * msg
    cnat = per * CAP
    cols = width // FOLD
    slots = peers * CAP
    xn = seq_n // 2
    me_z = lax.axis_index("dp")
    me_s = lax.axis_index("seq")
    me_h = lax.axis_index("head")
    me_x, me_c = me_s // 2, me_s % 2

    def at_offset(g, i, sign):
        dc, dh = i % 2, i // 2
        dx = (g + dh) % xn
        x = (me_x + sign * dx + xn) % xn
        return {"seq": x * 2 + (me_c + dc) % 2, "head": (me_h + sign * dh + head_n) % head_n}

    pairs = ((routes_hbm, routes), (mask_hbm, mask), (comb_hbm, comb), (gain_hbm, gain_v),
             (tok_hbm, tok), (wup_hbm.at[0], wup), (wdown_hbm.at[0], wdown))
    loads = [pltpu.make_async_copy(a, b, w_sem.at[i]) for i, (a, b) in enumerate(pairs)]
    for load in loads:
        load.start()

    barrier = pltpu.get_barrier_semaphore()

    def greet(j, _):
        x, h = (me_x + j // head_n) % xn, (me_h + j % head_n) % head_n
        pl.semaphore_signal(barrier, inc=1, device_id={"seq": x * 2 + 1, "head": h},
                            device_id_type=MESH)
        return _
    lax.fori_loop(me_c, peers // 2, greet, 0)
    mate = {"seq": me_x * 2 + 1 - me_c}

    @pl.when(me_c == 0)
    def _():
        def greet_z(j, _):
            pl.semaphore_signal(barrier, inc=1, device_id={"dp": (me_z + j) % dp_n},
                                device_id_type=MESH)
            return _
        lax.fori_loop(1, dp_n, greet_z, 0)

    def plane_ready():
        @pl.when(me_c == 1)
        def _():
            pl.semaphore_wait(barrier, peers - 1)
            pl.semaphore_signal(go, inc=1, device_id=mate, device_id_type=MESH)

        @pl.when(me_c == 0)
        def _():
            pl.semaphore_wait(go, 1)

    def to_mate(i, src, dst):
        return pltpu.make_async_remote_copy(src_ref=src, dst_ref=dst, send_sem=mate_send.at[i],
                                            recv_sem=mate_recv.at[i], device_id=mate,
                                            device_id_type=MESH)

    q, m = iota((crow, crow), 0), iota((crow, crow), 1)
    fold_m = (m == ((q // CAP) % FOLD) * cnat + (q // msg) * CAP + q % CAP).astype(BF16)
    back_m = (q == ((m // CAP) % FOLD) * cnat + (m // msg) * CAP + m % CAP).astype(BF16)

    def fold(block):
        stack = jnp.concatenate([block[:, c * cols:(c + 1) * cols] for c in range(FOLD)], axis=0)
        return dot(fold_m, stack).astype(BF16)

    def unfold(block):
        stack = dot(back_m, block).astype(BF16)
        return jnp.concatenate([stack[c * cnat:(c + 1) * cnat] for c in range(FOLD)], axis=1)

    def at(g, n):
        return pl.ds(pl.multiple_of(g * n, n), n)

    def start(phase, g, sign):
        def one(i, _):
            where = at(g * per + i, msg)
            pltpu.make_async_remote_copy(
                src_ref=snd.at[phase, where], dst_ref=rcv.at[phase, where],
                send_sem=send_sem.at[phase], recv_sem=recv_sem.at[phase, g],
                device_id=at_offset(g, i, sign), device_id_type=MESH).start()
            return _
        lax.fori_loop(1 if g == 0 else 0, per, one, 0)
        if g == 0:
            pltpu.make_async_copy(snd.at[phase, pl.ds(0, msg)], rcv.at[phase, pl.ds(0, msg)],
                                  recv_sem.at[phase, 0]).start()

    def arrived(phase, g):
        where = rcv.at[phase, at(g, crow)]
        pltpu.make_async_copy(where, where, recv_sem.at[phase, g]).wait()

    BR = 16

    for load in loads[:3]:
        load.wait()
    eye = iota((rows, rows), 0) == iota((rows, rows), 1)
    earlier = (iota((rows, rows), 0) < iota((rows, rows), 1)).astype(BF16)
    r0, r1 = routes[0:1, :], routes[1:2, :]
    experts = iota((peers, rows), 0)
    hot0, hot1 = (experts == r0).astype(F32), (experts == r1).astype(F32)
    before = dot((hot0 + hot1).astype(BF16), earlier)

    def slot_of(r, hot):
        turn = jnp.sum(before * hot, axis=0, keepdims=True).astype(I32)
        s, h = r // head_n, r % head_n
        dx = (s // 2 - me_x + xn) % xn
        dc = (s % 2 + me_c) % 2
        dh = (h - me_h + head_n) % head_n
        g = (dx - dh + head_n) % xn
        return (g * per + dh * 2 + dc) * CAP + turn

    def col_of(row):
        return jnp.sum(jnp.where(eye, row.astype(F32), 0.0), axis=1, keepdims=True)

    def as_row(col):
        return jnp.sum(jnp.where(eye, col, 0.0), axis=0, keepdims=True)

    s0_row, s1_row = slot_of(r0, hot0), slot_of(r1, hot1)
    s0, s1 = col_of(s0_row).astype(I32), col_of(s1_row).astype(I32)
    mask_col = col_of(mask[...])

    for load in loads[3:5]:
        load.wait()
    for k in range(width // 128):
        gain[:, k * 128:(k + 1) * 128] = gain_v[k:k + 1, :]

    def norm(b, _):
        r = at(b, BR)
        x = tok[r, :].astype(F32)
        inverse = lax.rsqrt(jnp.mean(x * x, axis=1, keepdims=True) + 1e-05)
        inv[r, :] = inverse
        nat[r, :] = (x * inverse * gain[...]).astype(BF16)
        return _
    lax.fori_loop(0, rows // BR, norm, 0)

    slot_lanes = iota((rows, slots), 1)
    pick0 = (slot_lanes == s0).astype(BF16)
    pick1 = (slot_lanes == s1).astype(BF16)
    sel[0:rows, :] = pick0
    sel[rows:2 * rows, :] = pick1

    def place(g):
        target = iota((cnat, rows), 0) + g * cnat
        return (target == s0_row).astype(BF16), (target == s1_row).astype(BF16)

    for g in range(CHUNKS):
        a, b = place(g)
        block = dot(a + b, nat[0:rows, :]).astype(BF16)
        snd[0, g * crow:(g + 1) * crow, :] = fold(block)
        if g == 0:
            plane_ready()
        start(0, g, 1)

    num[...] = jnp.broadcast_to(jnp.sum(mask_col, axis=0, keepdims=True), (8, 128))
    reduce_start(3, seq_n, me_s, "seq", num, cs, red_send, red_recv)
    for load in loads[5:]:
        load.wait()
    tile = 512
    tiles = width // tile

    for g in range(CHUNKS):
        arrived(0, g)
        r = slice(g * cnat, (g + 1) * cnat)
        xs[r, :] = unfold(rcv[0, g * crow:(g + 1) * crow, :])

        def up(n, _):
            c = at(n, tile)
            projected = dot(xs[r, :], wup[:, c])
            gate = jax.nn.sigmoid(1.702 * projected)
            slope[r, c] = gate + 1.702 * projected * gate * (1.0 - gate)
            nat[0:cnat, c] = (projected * gate).astype(BF16)
            return _
        lax.fori_loop(0, tiles, up, 0)

        def down(n, _):
            c = at(n, tile)
            nat[cnat:2 * cnat, c] = dot(nat[0:cnat, :], wdown[:, c]).astype(BF16)
            return _
        lax.fori_loop(0, tiles, down, 0)
        snd[1, g * crow:(g + 1) * crow, :] = fold(nat[cnat:2 * cnat, :])
        start(1, g, -1)

    num[...] = reduce_end(3, seq_n, cs, red_send, red_recv)
    reduce_start(4, head_n, me_h, "head", num, cy, red_send, red_recv)

    for g in range(CHUNKS):
        arrived(1, g)
        nat[g * cnat:(g + 1) * cnat, :] = unfold(rcv[1, g * crow:(g + 1) * crow, :])

    c0, c1 = col_of(comb[0:1, :]), col_of(comb[1:2, :])

    loss = jnp.zeros((rows, 1), F32)
    part0 = jnp.zeros((rows, 1), F32)
    part1 = jnp.zeros((rows, 1), F32)
    for n in range(tiles):
        c = slice(n * tile, (n + 1) * tile)
        both = dot(sel[...], nat[:, c])
        p0, p1 = both[0:rows], both[rows:2 * rows]
        mixed = tok[:, c].astype(F32) + c0 * p0 + c1 * p1
        cotangent = mask_col * mixed
        cot[:, c] = cotangent
        loss = loss + jnp.sum(cotangent * mixed, axis=1, keepdims=True)
        part0 = part0 + jnp.sum(cotangent * p0, axis=1, keepdims=True)
        part1 = part1 + jnp.sum(cotangent * p1, axis=1, keepdims=True)
        nat[0:rows, c] = (c0 * cotangent).astype(BF16)
        nat[rows:2 * rows, c] = (c1 * cotangent).astype(BF16)

    for g in range(CHUNKS):
        a, b = place(g)
        block = dot(jnp.concatenate([a, b], axis=1), nat[...]).astype(BF16)
        snd[2, g * crow:(g + 1) * crow, :] = fold(block)
        start(2, g, 1)

    num[...] = reduce_end(4, head_n, cy, red_send, red_recv)

    @pl.when(me_c == 0)
    def _():
        pl.semaphore_wait(barrier, dp_n - 1)
        reduce_start(5, dp_n, me_z, "dp", num, cz, red_send, red_recv)

    stats[...] = jnp.zeros_like(stats)
    stats[12:13, :] = jnp.broadcast_to(jnp.sum(loss, axis=0, keepdims=True), (1, 128))

    gain_part = [jnp.zeros((1, tile), F32) for _ in range(tiles)]
    for g in range(CHUNKS):
        arrived(2, g)
        r = slice(g * cnat, (g + 1) * cnat)
        nat[0:cnat, :] = unfold(rcv[2, g * crow:(g + 1) * crow, :])

        def down_t(n, _):
            c = at(n, tile)
            hidden_grad = lax.dot_general(nat[0:cnat, :], wdown[c, :], NT,
                                          preferred_element_type=F32)
            nat[cnat:2 * cnat, c] = (hidden_grad * slope[r, c]).astype(BF16)
            return _
        lax.fori_loop(0, tiles, down_t, 0)
        for n in range(tiles):
            c = slice(n * tile, (n + 1) * tile)
            row_grad = lax.dot_general(nat[cnat:2 * cnat, :], wup[c, :], NT,
                                       preferred_element_type=F32).astype(BF16)
            gain_part[n] = gain_part[n] + jnp.sum(
                row_grad.astype(F32) * xs[r, c].astype(F32), axis=0, keepdims=True)
            nat[2 * cnat:3 * cnat, c] = row_grad
        snd[3, g * crow:(g + 1) * crow, :] = fold(nat[2 * cnat:3 * cnat, :])
        if g == CHUNKS - 1:
            for n in range(tiles):
                for k in range(tile // 128):
                    at_k = n * (tile // 128) + k
                    stats[at_k:at_k + 1, :] = (
                        gain_part[n][:, k * 128:(k + 1) * 128]
                        / gain[:, at_k * 128:(at_k + 1) * 128])
            reduce_start(0, seq_n, me_s, "seq", stats, ars, red_send, red_recv)
        start(3, g, -1)

    stats[...] = reduce_end(0, seq_n, ars, red_send, red_recv)
    reduce_start(1, head_n, me_h, "head", stats, ary, red_send, red_recv)
    stats[...] = reduce_end(1, head_n, ary, red_send, red_recv)

    @pl.when(me_c == 0)
    def _():
        reduce_start(2, dp_n, me_z, "dp", stats, arz, red_send, red_recv)
        num_all[...] = reduce_end(5, dp_n, cz, red_send, red_recv)
        copy = to_mate(0, num_all, num_all)
        copy.start()
        copy.wait_send()

    @pl.when(me_c == 1)
    def _():
        to_mate(0, num_all, num_all).wait_recv()

    count = num_all[0:1, 0:1]
    ratio = (rows * dp_n * peers) / count
    out_comb[0:1, :] = ratio * as_row(part0)
    out_comb[1:2, :] = ratio * as_row(part1)
    sel[0:rows, :] = sel[0:rows, :] + sel[rows:2 * rows, :]

    for g in range(CHUNKS):
        arrived(3, g)
        nat[g * cnat:(g + 1) * cnat, :] = unfold(rcv[3, g * crow:(g + 1) * crow, :])
    for n in range(tiles):
        c = slice(n * tile, (n + 1) * tile)
        slope[0:rows, c] = dot(sel[0:rows, :], nat[:, c])

    def last(b, _):
        r = at(b, BR)
        inverse = inv[r, :]
        normed = tok[r, :].astype(F32) * inverse
        grad = slope[r, :] * gain[...]
        mean = jnp.mean(grad * normed, axis=1, keepdims=True)
        tok[r, :] = (ratio * (cot[r, :] + inverse * (grad - normed * mean))).astype(BF16)
        return _
    lax.fori_loop(0, rows // BR, last, 0)
    leave = pltpu.make_async_copy(tok, out_tok, w_sem.at[7])
    leave.start()

    for phase in range(4):
        sent = snd.at[phase, pl.ds(msg, (peers - 1) * msg)]
        pltpu.make_async_copy(sent, sent, send_sem.at[phase]).wait()

    @pl.when(me_c == 0)
    def _():
        stats_all[...] = reduce_end(2, dp_n, arz, red_send, red_recv)
        copy = to_mate(1, stats_all, stats_all)
        copy.start()
        copy.wait_send()

    @pl.when(me_c == 1)
    def _():
        to_mate(1, stats_all, stats_all).wait_recv()

    leave.wait()
    out_gain[...] = stats_all[0:width // 128, :] / count
    out_loss[...] = stats_all[12:13, 0:1] / (2.0 * width * count)


def reduce_start(stage, n, me, axis, stats, parts, send_sem, recv_sem):
    parts[pl.ds(n, 1)] = stats[...][None]
    parts[pl.ds(me, 1)] = stats[...][None]

    def one(j, _):
        pltpu.make_async_remote_copy(
            src_ref=parts.at[pl.ds(n, 1)], dst_ref=parts.at[pl.ds(me, 1)],
            send_sem=send_sem.at[stage], recv_sem=recv_sem.at[stage],
            device_id={axis: (me + j) % n}, device_id_type=MESH).start()
        return _
    lax.fori_loop(1, n, one, 0)


def reduce_end(stage, n, parts, send_sem, recv_sem):
    where = parts.at[pl.ds(0, n - 1)]
    pltpu.make_async_copy(where, where, recv_sem.at[stage]).wait()
    pltpu.make_async_copy(where, where, send_sem.at[stage]).wait()
    total = parts[0]
    for k in range(1, n):
        total = total + parts[k]
    return total


def solution(mesh):
    sizes = (mesh.shape["dp"], mesh.shape["seq"], mesh.shape["head"])

    def on_device(tokens, norm_gain, w_up, w_down, routes, combine, loss_mask):
        rows, width = tokens.shape
        peers = sizes[1] * sizes[2]
        slots = peers * CAP
        folded = (4, slots * FOLD, width // FOLD)
        vmem = pl.BlockSpec(memory_space=pltpu.VMEM)
        hbm = pl.BlockSpec(memory_space=pltpu.HBM)
        grad_tokens, grad_gain, grad_combine, loss = pl.pallas_call(
            lambda *refs: kernel(sizes, *refs),
            out_shape=(
                jax.ShapeDtypeStruct((rows, width), BF16),
                jax.ShapeDtypeStruct((width // 128, 128), F32),
                jax.ShapeDtypeStruct((2, rows), F32),
                jax.ShapeDtypeStruct((1, 1), F32),
            ),
            in_specs=[hbm] * 7,
            out_specs=(hbm, vmem, vmem, vmem),
            scratch_shapes=[
                pltpu.VMEM((rows, width), BF16),
                pltpu.VMEM((width // 128, 128), F32),
                pltpu.VMEM((2, rows), I32),
                pltpu.VMEM((2, rows), F32),
                pltpu.VMEM((1, rows), I32),
                pltpu.VMEM((1, width), F32),
                pltpu.VMEM((rows, 1), F32),
                pltpu.VMEM(w_up.shape[1:], BF16),
                pltpu.VMEM(w_down.shape[1:], BF16),
                pltpu.VMEM(folded, BF16),
                pltpu.VMEM(folded, BF16),
                pltpu.VMEM((slots, width), BF16),
                pltpu.VMEM((slots, width), F32),
                pltpu.VMEM((slots, width), BF16),
                pltpu.VMEM((2 * rows, slots), BF16),
                pltpu.VMEM((rows, width), F32),
                pltpu.VMEM((16, 128), F32),
                pltpu.VMEM((sizes[0] + 1, 16, 128), F32),
                pltpu.VMEM((sizes[1] + 1, 16, 128), F32),
                pltpu.VMEM((sizes[2] + 1, 16, 128), F32),
                pltpu.VMEM((8, 128), F32),
                pltpu.VMEM((sizes[0] + 1, 8, 128), F32),
                pltpu.VMEM((sizes[1] + 1, 8, 128), F32),
                pltpu.VMEM((sizes[2] + 1, 8, 128), F32),
                pltpu.VMEM((16, 128), F32),
                pltpu.VMEM((8, 128), F32),
                pltpu.SemaphoreType.DMA((4,)),
                pltpu.SemaphoreType.DMA((4, CHUNKS)),
                pltpu.SemaphoreType.DMA((8,)),
                pltpu.SemaphoreType.DMA((6,)),
                pltpu.SemaphoreType.DMA((6,)),
                pltpu.SemaphoreType.REGULAR,
                pltpu.SemaphoreType.DMA((2,)),
                pltpu.SemaphoreType.DMA((2,)),
            ],
            compiler_params=pltpu.CompilerParams(
                collective_id=1, has_side_effects=True, vmem_limit_bytes=60 * 2**20),
            cost_estimate=pl.CostEstimate(
                flops=8 * slots * width * width, bytes_accessed=4 * width * width,
                transcendentals=slots * width),
            name="moe",
        )(tokens, norm_gain.reshape(width // 128, 128), w_up, w_down, routes.T, combine.T,
          loss_mask.reshape(1, rows))
        return grad_tokens, grad_gain.reshape(width), grad_combine.T, loss.reshape(())

    split = ("dp", "seq", "head")
    in_specs = (P(split, None), P(), P(("seq", "head"), None, None), P(("seq", "head"), None, None),
                P(split, None), P(split, None), P(split))
    out_specs = (P(split, None), P(), P(split, None), P())
    return jax.shard_map(on_device, mesh=mesh, in_specs=in_specs, out_specs=out_specs,
                         check_vma=False)
```

```python
import jax
import jax.numpy as jnp
from jax import lax
from jax.experimental import pallas as pl
from jax.experimental.pallas import tpu as pltpu
from jax.sharding import PartitionSpec as P

F32, BF16, I32 = jnp.float32, jnp.bfloat16, jnp.int32
MESH = pl.DeviceIdType.MESH
CAP = 4
FOLD = 4
CHUNKS = 4
HELD = 2
NT = (((1,), (1,)), ((), ()))


def dot(a, b):
    return jnp.dot(a, b, preferred_element_type=F32)


def iota(shape, dim):
    return lax.broadcasted_iota(I32, shape, dim)


def kernel(sizes, tok_hbm, gain_hbm, wup_hbm, wdown_hbm, routes_hbm, comb_hbm, mask_hbm,
           out_tok, out_gain, out_comb, out_loss,
           tok, gain_v, routes, comb, mask, gain, inv,
           wup, wdown, snd, rcv, xs, slope, nat, sel, cot, stats, arz, ars, ary, num, cz, cs, cy,
           stats_all, num_all,
           send_sem, recv_sem, w_sem, red_send, red_recv, go, mate_send, mate_recv):
    dp_n, seq_n, head_n = sizes
    rows, width = tok.shape
    peers = seq_n * head_n
    per = peers // CHUNKS
    msg = CAP * FOLD
    crow = per * msg
    cnat = per * CAP
    cols = width // FOLD
    slots = peers * CAP
    xn = seq_n // 2
    me_z = lax.axis_index("dp")
    me_s = lax.axis_index("seq")
    me_h = lax.axis_index("head")
    me_x, me_c = me_s // 2, me_s % 2

    def at_offset(g, i, sign):
        dc, dh = i % 2, i // 2
        dx = (g + dh) % xn
        x = (me_x + sign * dx + xn) % xn
        return {"seq": x * 2 + (me_c + dc) % 2, "head": (me_h + sign * dh + head_n) % head_n}

    pairs = ((routes_hbm, routes), (mask_hbm, mask), (comb_hbm, comb), (gain_hbm, gain_v),
             (tok_hbm, tok), (wup_hbm.at[0], wup), (wdown_hbm.at[0], wdown))
    loads = [pltpu.make_async_copy(a, b, w_sem.at[i]) for i, (a, b) in enumerate(pairs)]
    for load in loads:
        load.start()

    barrier = pltpu.get_barrier_semaphore()

    def greet(j, _):
        x, h = (me_x + j // head_n) % xn, (me_h + j % head_n) % head_n
        pl.semaphore_signal(barrier, inc=1, device_id={"seq": x * 2 + 1, "head": h},
                            device_id_type=MESH)
        return _
    lax.fori_loop(me_c, peers // 2, greet, 0)
    mate = {"seq": me_x * 2 + 1 - me_c}

    @pl.when(me_c == 0)
    def _():
        def greet_z(j, _):
            pl.semaphore_signal(barrier, inc=1, device_id={"dp": (me_z + j) % dp_n},
                                device_id_type=MESH)
            return _
        lax.fori_loop(1, dp_n, greet_z, 0)

    def plane_ready():
        @pl.when(me_c == 1)
        def _():
            pl.semaphore_wait(barrier, peers - 1)
            pl.semaphore_signal(go, inc=1, device_id=mate, device_id_type=MESH)

        @pl.when(me_c == 0)
        def _():
            pl.semaphore_wait(go, 1)

    def to_mate(i, src, dst):
        return pltpu.make_async_remote_copy(src_ref=src, dst_ref=dst, send_sem=mate_send.at[i],
                                            recv_sem=mate_recv.at[i], device_id=mate,
                                            device_id_type=MESH)

    q, m = iota((crow, crow), 0), iota((crow, crow), 1)
    fold_m = (m == ((q // CAP) % FOLD) * cnat + (q // msg) * CAP + q % CAP).astype(BF16)
    back_m = (q == ((m // CAP) % FOLD) * cnat + (m // msg) * CAP + m % CAP).astype(BF16)

    def fold(block):
        stack = jnp.concatenate([block[:, c * cols:(c + 1) * cols] for c in range(FOLD)], axis=0)
        return dot(fold_m, stack).astype(BF16)

    def unfold(block):
        stack = dot(back_m, block).astype(BF16)
        return jnp.concatenate([stack[c * cnat:(c + 1) * cnat] for c in range(FOLD)], axis=1)

    def at(g, n):
        return pl.ds(pl.multiple_of(g * n, n), n)

    def start(phase, g, sign):
        def one(i, _):
            where = at(g * per + i, msg)
            pltpu.make_async_remote_copy(
                src_ref=snd.at[phase, where], dst_ref=rcv.at[phase, where],
                send_sem=send_sem.at[phase], recv_sem=recv_sem.at[phase, g],
                device_id=at_offset(g, i, sign), device_id_type=MESH).start()
            return _
        lax.fori_loop(1 if g == 0 else 0, per, one, 0)
        if g == 0:
            pltpu.make_async_copy(snd.at[phase, pl.ds(0, msg)], rcv.at[phase, pl.ds(0, msg)],
                                  recv_sem.at[phase, 0]).start()

    def arrived(phase, g):
        where = rcv.at[phase, at(g, crow)]
        pltpu.make_async_copy(where, where, recv_sem.at[phase, g]).wait()

    BR = 16

    for load in loads[:3]:
        load.wait()
    eye = iota((rows, rows), 0) == iota((rows, rows), 1)
    earlier = (iota((rows, rows), 0) < iota((rows, rows), 1)).astype(BF16)
    r0, r1 = routes[0:1, :], routes[1:2, :]
    experts = iota((peers, rows), 0)
    hot0, hot1 = (experts == r0).astype(F32), (experts == r1).astype(F32)
    before = dot((hot0 + hot1).astype(BF16), earlier)

    def slot_of(r, hot):
        turn = jnp.sum(before * hot, axis=0, keepdims=True).astype(I32)
        s, h = r // head_n, r % head_n
        dx = (s // 2 - me_x + xn) % xn
        dc = (s % 2 + me_c) % 2
        dh = (h - me_h + head_n) % head_n
        g = (dx - dh + head_n) % xn
        return (g * per + dh * 2 + dc) * CAP + turn

    def col_of(row):
        return jnp.sum(jnp.where(eye, row.astype(F32), 0.0), axis=1, keepdims=True)

    def as_row(col):
        return jnp.sum(jnp.where(eye, col, 0.0), axis=0, keepdims=True)

    s0_row, s1_row = slot_of(r0, hot0), slot_of(r1, hot1)
    s0, s1 = col_of(s0_row).astype(I32), col_of(s1_row).astype(I32)
    mask_col = col_of(mask[...])

    for load in loads[3:5]:
        load.wait()
    for k in range(width // 128):
        gain[:, k * 128:(k + 1) * 128] = gain_v[k:k + 1, :]

    def norm(b, _):
        r = at(b, BR)
        x = tok[r, :].astype(F32)
        inverse = lax.rsqrt(jnp.mean(x * x, axis=1, keepdims=True) + 1e-05)
        inv[r, :] = inverse
        nat[r, :] = (x * inverse * gain[...]).astype(BF16)
        return _
    lax.fori_loop(0, rows // BR, norm, 0)

    slot_lanes = iota((rows, slots), 1)
    pick0 = (slot_lanes == s0).astype(BF16)
    pick1 = (slot_lanes == s1).astype(BF16)
    sel[0:rows, :] = pick0
    sel[rows:2 * rows, :] = pick1

    def place(g):
        target = iota((cnat, rows), 0) + g * cnat
        return (target == s0_row).astype(BF16), (target == s1_row).astype(BF16)

    for g in range(CHUNKS):
        a, b = place(g)
        block = dot(a + b, nat[0:rows, :]).astype(BF16)
        snd[0, g * crow:(g + 1) * crow, :] = fold(block)
        if g == 0:
            plane_ready()
        start(0, g, 1)

    num[...] = jnp.broadcast_to(jnp.sum(mask_col, axis=0, keepdims=True), (8, 128))
    reduce_start(3, seq_n, me_s, "seq", num, cs, red_send, red_recv)
    for load in loads[5:]:
        load.wait()
    tile = 512
    tiles = width // tile

    for g in range(CHUNKS):
        arrived(0, g)
        r = slice(g * cnat, (g + 1) * cnat)
        xs[r, :] = unfold(rcv[0, g * crow:(g + 1) * crow, :])

        def up(n, _):
            c = at(n, tile)
            projected = dot(xs[r, :], wup[:, c])
            gate = jax.nn.sigmoid(1.702 * projected)
            slope[r, c] = gate + 1.702 * projected * gate * (1.0 - gate)
            nat[0:cnat, c] = (projected * gate).astype(BF16)
            return _
        lax.fori_loop(0, tiles, up, 0)

        def down(n, _):
            c = at(n, tile)
            nat[cnat:2 * cnat, c] = dot(nat[0:cnat, :], wdown[:, c]).astype(BF16)
            return _
        lax.fori_loop(0, tiles, down, 0)
        snd[1, g * crow:(g + 1) * crow, :] = fold(nat[cnat:2 * cnat, :])
        start(1, g, -1)

    num[...] = reduce_end(3, seq_n, cs, red_send, red_recv)
    reduce_start(4, head_n, me_h, "head", num, cy, red_send, red_recv)

    for g in range(CHUNKS):
        arrived(1, g)
        nat[g * cnat:(g + 1) * cnat, :] = unfold(rcv[1, g * crow:(g + 1) * crow, :])

    c0, c1 = col_of(comb[0:1, :]), col_of(comb[1:2, :])

    loss = jnp.zeros((rows, 1), F32)
    part0 = jnp.zeros((rows, 1), F32)
    part1 = jnp.zeros((rows, 1), F32)
    for n in range(tiles):
        c = slice(n * tile, (n + 1) * tile)
        both = dot(sel[...], nat[:, c])
        p0, p1 = both[0:rows], both[rows:2 * rows]
        mixed = tok[:, c].astype(F32) + c0 * p0 + c1 * p1
        cotangent = mask_col * mixed
        cot[:, c] = cotangent
        loss = loss + jnp.sum(cotangent * mixed, axis=1, keepdims=True)
        part0 = part0 + jnp.sum(cotangent * p0, axis=1, keepdims=True)
        part1 = part1 + jnp.sum(cotangent * p1, axis=1, keepdims=True)
        nat[0:rows, c] = (c0 * cotangent).astype(BF16)
        nat[rows:2 * rows, c] = (c1 * cotangent).astype(BF16)

    for g in range(CHUNKS):
        a, b = place(g)
        block = dot(jnp.concatenate([a, b], axis=1), nat[...]).astype(BF16)
        snd[2, g * crow:(g + 1) * crow, :] = fold(block)
        start(2, g, 1)

    num[...] = reduce_end(4, head_n, cy, red_send, red_recv)

    @pl.when(me_c == 0)
    def _():
        pl.semaphore_wait(barrier, dp_n - 1)
        reduce_start(5, dp_n, me_z, "dp", num, cz, red_send, red_recv)

    stats[...] = jnp.zeros_like(stats)
    stats[12:13, :] = jnp.broadcast_to(jnp.sum(loss, axis=0, keepdims=True), (1, 128))

    gain_part = [jnp.zeros((1, tile), F32) for _ in range(tiles)]
    for g in range(CHUNKS):
        arrived(2, g)
        r = slice(g * cnat, (g + 1) * cnat)
        nat[0:cnat, :] = unfold(rcv[2, g * crow:(g + 1) * crow, :])

        def down_t(n, _):
            c = at(n, tile)
            hidden_grad = lax.dot_general(nat[0:cnat, :], wdown[c, :], NT,
                                          preferred_element_type=F32)
            nat[cnat:2 * cnat, c] = (hidden_grad * slope[r, c]).astype(BF16)
            return _
        lax.fori_loop(0, tiles, down_t, 0)
        for n in range(tiles):
            c = slice(n * tile, (n + 1) * tile)
            row_grad = lax.dot_general(nat[cnat:2 * cnat, :], wup[c, :], NT,
                                       preferred_element_type=F32).astype(BF16)
            gain_part[n] = gain_part[n] + jnp.sum(
                row_grad.astype(F32) * xs[r, c].astype(F32), axis=0, keepdims=True)
            nat[2 * cnat:3 * cnat, c] = row_grad
        snd[3, g * crow:(g + 1) * crow, :] = fold(nat[2 * cnat:3 * cnat, :])
        if g == CHUNKS - 1:
            for n in range(tiles):
                for k in range(tile // 128):
                    at_k = n * (tile // 128) + k
                    stats[at_k:at_k + 1, :] = (
                        gain_part[n][:, k * 128:(k + 1) * 128]
                        / gain[:, at_k * 128:(at_k + 1) * 128])
            reduce_start(0, seq_n, me_s, "seq", stats, ars, red_send, red_recv)
        if g < CHUNKS - HELD:
            start(3, g, -1)

    stats[...] = reduce_end(0, seq_n, ars, red_send, red_recv)
    reduce_start(1, head_n, me_h, "head", stats, ary, red_send, red_recv)
    for g in range(CHUNKS - HELD, CHUNKS):
        start(3, g, -1)
    stats[...] = reduce_end(1, head_n, ary, red_send, red_recv)

    @pl.when(me_c == 0)
    def _():
        reduce_start(2, dp_n, me_z, "dp", stats, arz, red_send, red_recv)
        num_all[...] = reduce_end(5, dp_n, cz, red_send, red_recv)
        copy = to_mate(0, num_all, num_all)
        copy.start()
        copy.wait_send()

    @pl.when(me_c == 1)
    def _():
        to_mate(0, num_all, num_all).wait_recv()

    count = num_all[0:1, 0:1]
    ratio = (rows * dp_n * peers) / count
    out_comb[0:1, :] = ratio * as_row(part0)
    out_comb[1:2, :] = ratio * as_row(part1)
    sel[0:rows, :] = sel[0:rows, :] + sel[rows:2 * rows, :]

    for g in range(CHUNKS):
        arrived(3, g)
        nat[g * cnat:(g + 1) * cnat, :] = unfold(rcv[3, g * crow:(g + 1) * crow, :])
    for n in range(tiles):
        c = slice(n * tile, (n + 1) * tile)
        slope[0:rows, c] = dot(sel[0:rows, :], nat[:, c])

    def last(b, _):
        r = at(b, BR)
        inverse = inv[r, :]
        normed = tok[r, :].astype(F32) * inverse
        grad = slope[r, :] * gain[...]
        mean = jnp.mean(grad * normed, axis=1, keepdims=True)
        out_tok[r, :] = (ratio * (cot[r, :] + inverse * (grad - normed * mean))).astype(BF16)
        return _
    lax.fori_loop(0, rows // BR, last, 0)

    for phase in range(4):
        sent = snd.at[phase, pl.ds(msg, (peers - 1) * msg)]
        pltpu.make_async_copy(sent, sent, send_sem.at[phase]).wait()

    @pl.when(me_c == 0)
    def _():
        stats_all[...] = reduce_end(2, dp_n, arz, red_send, red_recv)
        copy = to_mate(1, stats_all, stats_all)
        copy.start()
        copy.wait_send()

    @pl.when(me_c == 1)
    def _():
        to_mate(1, stats_all, stats_all).wait_recv()

    out_gain[...] = stats_all[0:width // 128, :] / count
    out_loss[...] = stats_all[12:13, 0:1] / (2.0 * width * count)


def reduce_start(stage, n, me, axis, stats, parts, send_sem, recv_sem):
    parts[pl.ds(n, 1)] = stats[...][None]
    parts[pl.ds(me, 1)] = stats[...][None]

    def one(j, _):
        pltpu.make_async_remote_copy(
            src_ref=parts.at[pl.ds(n, 1)], dst_ref=parts.at[pl.ds(me, 1)],
            send_sem=send_sem.at[stage], recv_sem=recv_sem.at[stage],
            device_id={axis: (me + j) % n}, device_id_type=MESH).start()
        return _
    lax.fori_loop(1, n, one, 0)


def reduce_end(stage, n, parts, send_sem, recv_sem):
    where = parts.at[pl.ds(0, n - 1)]
    pltpu.make_async_copy(where, where, recv_sem.at[stage]).wait()
    pltpu.make_async_copy(where, where, send_sem.at[stage]).wait()
    total = parts[0]
    for k in range(1, n):
        total = total + parts[k]
    return total


def solution(mesh):
    sizes = (mesh.shape["dp"], mesh.shape["seq"], mesh.shape["head"])

    def on_device(tokens, norm_gain, w_up, w_down, routes, combine, loss_mask):
        rows, width = tokens.shape
        peers = sizes[1] * sizes[2]
        slots = peers * CAP
        folded = (4, slots * FOLD, width // FOLD)
        vmem = pl.BlockSpec(memory_space=pltpu.VMEM)
        hbm = pl.BlockSpec(memory_space=pltpu.HBM)
        keep = lambda x: pltpu.with_memory_space_constraint(x, pltpu.HBM)
        grad_tokens, grad_gain, grad_combine, loss = pl.pallas_call(
            lambda *refs: kernel(sizes, *refs),
            out_shape=(
                jax.ShapeDtypeStruct((rows, width), BF16),
                jax.ShapeDtypeStruct((width // 128, 128), F32),
                jax.ShapeDtypeStruct((2, rows), F32),
                jax.ShapeDtypeStruct((1, 1), F32),
            ),
            in_specs=[hbm] * 7,
            out_specs=(vmem, vmem, vmem, vmem),
            scratch_shapes=[
                pltpu.VMEM((rows, width), BF16),
                pltpu.VMEM((width // 128, 128), F32),
                pltpu.VMEM((2, rows), I32),
                pltpu.VMEM((2, rows), F32),
                pltpu.VMEM((1, rows), I32),
                pltpu.VMEM((1, width), F32),
                pltpu.VMEM((rows, 1), F32),
                pltpu.VMEM(w_up.shape[1:], BF16),
                pltpu.VMEM(w_down.shape[1:], BF16),
                pltpu.VMEM(folded, BF16),
                pltpu.VMEM(folded, BF16),
                pltpu.VMEM((slots, width), BF16),
                pltpu.VMEM((slots, width), F32),
                pltpu.VMEM((slots, width), BF16),
                pltpu.VMEM((2 * rows, slots), BF16),
                pltpu.VMEM((rows, width), F32),
                pltpu.VMEM((16, 128), F32),
                pltpu.VMEM((sizes[0] + 1, 16, 128), F32),
                pltpu.VMEM((sizes[1] + 1, 16, 128), F32),
                pltpu.VMEM((sizes[2] + 1, 16, 128), F32),
                pltpu.VMEM((8, 128), F32),
                pltpu.VMEM((sizes[0] + 1, 8, 128), F32),
                pltpu.VMEM((sizes[1] + 1, 8, 128), F32),
                pltpu.VMEM((sizes[2] + 1, 8, 128), F32),
                pltpu.VMEM((16, 128), F32),
                pltpu.VMEM((8, 128), F32),
                pltpu.SemaphoreType.DMA((4,)),
                pltpu.SemaphoreType.DMA((4, CHUNKS)),
                pltpu.SemaphoreType.DMA((8,)),
                pltpu.SemaphoreType.DMA((6,)),
                pltpu.SemaphoreType.DMA((6,)),
                pltpu.SemaphoreType.REGULAR,
                pltpu.SemaphoreType.DMA((2,)),
                pltpu.SemaphoreType.DMA((2,)),
            ],
            compiler_params=pltpu.CompilerParams(
                collective_id=1, has_side_effects=True, vmem_limit_bytes=48 * 2**20),
            cost_estimate=pl.CostEstimate(
                flops=8 * slots * width * width, bytes_accessed=4 * width * width,
                transcendentals=slots * width),
            name="moe",
        )(*map(keep, (tokens, norm_gain.reshape(width // 128, 128), w_up, w_down, routes.T,
                      combine.T, loss_mask.reshape(1, rows))))
        return grad_tokens, grad_gain.reshape(width), grad_combine.T, loss.reshape(())

    split = ("dp", "seq", "head")
    in_specs = (P(split, None), P(), P(("seq", "head"), None, None), P(("seq", "head"), None, None),
                P(split, None), P(split, None), P(split))
    out_specs = (P(split, None), P(), P(split, None), P())
    return jax.shard_map(on_device, mesh=mesh, in_specs=in_specs, out_specs=out_specs,
                         check_vma=False)
```

```python
import jax
import jax.numpy as jnp
from jax import lax
from jax.experimental import pallas as pl
from jax.experimental.pallas import tpu as pltpu
from jax.sharding import PartitionSpec as P

F32, BF16, I32 = jnp.float32, jnp.bfloat16, jnp.int32
MESH = pl.DeviceIdType.MESH
CAP = 4
FOLD = 4
CHUNKS = 4
HELD = 2


def dot(a, b):
    return jnp.dot(a, b, preferred_element_type=F32)


def iota(shape, dim):
    return lax.broadcasted_iota(I32, shape, dim)


def kernel(sizes, tok_hbm, gain_hbm, wup_hbm, wdown_hbm, routes_hbm, comb_hbm, mask_hbm,
           out_tok, out_gain, out_comb, out_loss,
           tok, gain_v, routes, comb, mask, gain, inv,
           wup, wdown, wup_t, wdown_t, snd, rcv, xs, slope, nat, sel, cot, stats, arz, ars, ary, num, cz, cs, cy,
           stats_all, num_all,
           send_sem, recv_sem, w_sem, red_send, red_recv, go, mate_send, mate_recv):
    dp_n, seq_n, head_n = sizes
    rows, width = tok.shape
    peers = seq_n * head_n
    per = peers // CHUNKS
    msg = CAP * FOLD
    crow = per * msg
    cnat = per * CAP
    cols = width // FOLD
    slots = peers * CAP
    xn = seq_n // 2
    me_z = lax.axis_index("dp")
    me_s = lax.axis_index("seq")
    me_h = lax.axis_index("head")
    me_x, me_c = me_s // 2, me_s % 2

    def at_offset(g, i, sign):
        dc, dh = i % 2, i // 2
        dx = (g + dh) % xn
        x = (me_x + sign * dx + xn) % xn
        return {"seq": x * 2 + (me_c + dc) % 2, "head": (me_h + sign * dh + head_n) % head_n}

    pairs = ((routes_hbm, routes), (mask_hbm, mask), (comb_hbm, comb), (gain_hbm, gain_v),
             (tok_hbm, tok), (wup_hbm.at[0], wup), (wdown_hbm.at[0], wdown))
    loads = [pltpu.make_async_copy(a, b, w_sem.at[i]) for i, (a, b) in enumerate(pairs)]
    for load in loads:
        load.start()

    barrier = pltpu.get_barrier_semaphore()

    def greet(j, _):
        x, h = (me_x + j // head_n) % xn, (me_h + j % head_n) % head_n
        pl.semaphore_signal(barrier, inc=1, device_id={"seq": x * 2 + 1, "head": h},
                            device_id_type=MESH)
        return _
    lax.fori_loop(me_c, peers // 2, greet, 0)
    mate = {"seq": me_x * 2 + 1 - me_c}

    def plane_ready():
        @pl.when(me_c == 1)
        def _():
            pl.semaphore_wait(barrier, peers - 1)
            pl.semaphore_signal(go, inc=1, device_id=mate, device_id_type=MESH)

        @pl.when(me_c == 0)
        def _():
            pl.semaphore_wait(go, 1)

    def to_mate(i, src, dst):
        return pltpu.make_async_remote_copy(src_ref=src, dst_ref=dst, send_sem=mate_send.at[i],
                                            recv_sem=mate_recv.at[i], device_id=mate,
                                            device_id_type=MESH)

    q, m = iota((crow, crow), 0), iota((crow, crow), 1)
    fold_m = (m == ((q // CAP) % FOLD) * cnat + (q // msg) * CAP + q % CAP).astype(BF16)
    back_m = (q == ((m // CAP) % FOLD) * cnat + (m // msg) * CAP + m % CAP).astype(BF16)

    def fold(block):
        stack = jnp.concatenate([block[:, c * cols:(c + 1) * cols] for c in range(FOLD)], axis=0)
        return dot(fold_m, stack).astype(BF16)

    def unfold(block):
        stack = dot(back_m, block).astype(BF16)
        return jnp.concatenate([stack[c * cnat:(c + 1) * cnat] for c in range(FOLD)], axis=1)

    def at(g, n):
        return pl.ds(pl.multiple_of(g * n, n), n)

    def start(phase, g, sign):
        def one(i, _):
            where = at(g * per + i, msg)
            pltpu.make_async_remote_copy(
                src_ref=snd.at[phase, where], dst_ref=rcv.at[phase, where],
                send_sem=send_sem.at[phase], recv_sem=recv_sem.at[phase, g],
                device_id=at_offset(g, i, sign), device_id_type=MESH).start()
            return _
        lax.fori_loop(1 if g == 0 else 0, per, one, 0)
        if g == 0:
            pltpu.make_async_copy(snd.at[phase, pl.ds(0, msg)], rcv.at[phase, pl.ds(0, msg)],
                                  recv_sem.at[phase, 0]).start()

    def arrived(phase, g):
        where = rcv.at[phase, at(g, crow)]
        pltpu.make_async_copy(where, where, recv_sem.at[phase, g]).wait()

    BR = 16

    for load in loads[:3]:
        load.wait()
    eye = iota((rows, rows), 0) == iota((rows, rows), 1)
    earlier = (iota((rows, rows), 0) < iota((rows, rows), 1)).astype(BF16)
    r0, r1 = routes[0:1, :], routes[1:2, :]
    experts = iota((peers, rows), 0)
    hot0, hot1 = (experts == r0).astype(F32), (experts == r1).astype(F32)
    before = dot((hot0 + hot1).astype(BF16), earlier)

    def slot_of(r, hot):
        turn = jnp.sum(before * hot, axis=0, keepdims=True).astype(I32)
        s, h = r // head_n, r % head_n
        dx = (s // 2 - me_x + xn) % xn
        dc = (s % 2 + me_c) % 2
        dh = (h - me_h + head_n) % head_n
        g = (dx - dh + head_n) % xn
        return (g * per + dh * 2 + dc) * CAP + turn

    def col_of(row):
        return jnp.sum(jnp.where(eye, row.astype(F32), 0.0), axis=1, keepdims=True)

    def as_row(col):
        return jnp.sum(jnp.where(eye, col, 0.0), axis=0, keepdims=True)

    s0_row, s1_row = slot_of(r0, hot0), slot_of(r1, hot1)
    s0, s1 = col_of(s0_row).astype(I32), col_of(s1_row).astype(I32)
    mask_col = col_of(mask[...])

    for load in loads[3:5]:
        load.wait()
    for k in range(width // 128):
        gain[:, k * 128:(k + 1) * 128] = gain_v[k:k + 1, :]

    def norm(b, _):
        r = at(b, BR)
        x = tok[r, :].astype(F32)
        inverse = lax.rsqrt(jnp.mean(x * x, axis=1, keepdims=True) + 1e-05)
        inv[r, :] = inverse
        nat[r, :] = (x * inverse * gain[...]).astype(BF16)
        return _
    lax.fori_loop(0, rows // BR, norm, 0)

    slot_lanes = iota((rows, slots), 1)
    pick0 = (slot_lanes == s0).astype(BF16)
    pick1 = (slot_lanes == s1).astype(BF16)
    sel[0:rows, :] = pick0
    sel[rows:2 * rows, :] = pick1

    def place(g):
        target = iota((cnat, rows), 0) + g * cnat
        return (target == s0_row).astype(BF16), (target == s1_row).astype(BF16)

    for g in range(CHUNKS):
        a, b = place(g)
        block = dot(a + b, nat[0:rows, :]).astype(BF16)
        snd[0, g * crow:(g + 1) * crow, :] = fold(block)
        if g == 0:
            plane_ready()
        start(0, g, 1)

    @pl.when(me_c == 0)
    def _():
        def greet_z(j, _):
            pl.semaphore_signal(barrier, inc=1, device_id={"dp": (me_z + j) % dp_n},
                                device_id_type=MESH)
            return _
        lax.fori_loop(1, dp_n, greet_z, 0)

    num[...] = jnp.broadcast_to(jnp.sum(mask_col, axis=0, keepdims=True), (8, 128))
    reduce_start(3, seq_n, me_s, "seq", num, cs, red_send, red_recv)
    for load in loads[5:]:
        load.wait()
    tile = 768
    tiles = width // tile
    edge = 256
    blocks = width // edge

    def turn(i, _):
        a, b = at(i // blocks, edge), at(i % blocks, edge)
        wdown_t[b, a] = wdown[a, b].T
        wup_t[b, a] = wup[a, b].T
        return _
    lax.fori_loop(0, blocks * blocks, turn, 0)

    for g in range(CHUNKS):
        arrived(0, g)
        r = slice(g * cnat, (g + 1) * cnat)
        xs[r, :] = unfold(rcv[0, g * crow:(g + 1) * crow, :])

        def up(n, _):
            c = at(n, tile)
            projected = dot(xs[r, :], wup[:, c])
            gate = jax.nn.sigmoid(1.702 * projected)
            slope[r, c] = gate + 1.702 * projected * gate * (1.0 - gate)
            nat[0:cnat, c] = (projected * gate).astype(BF16)
            return _
        lax.fori_loop(0, tiles, up, 0)

        def down(n, _):
            c = at(n, tile)
            nat[cnat:2 * cnat, c] = dot(nat[0:cnat, :], wdown[:, c]).astype(BF16)
            return _
        lax.fori_loop(0, tiles, down, 0)
        snd[1, g * crow:(g + 1) * crow, :] = fold(nat[cnat:2 * cnat, :])
        start(1, g, -1)

    num[...] = reduce_end(3, seq_n, cs, red_send, red_recv)
    reduce_start(4, head_n, me_h, "head", num, cy, red_send, red_recv)

    for g in range(CHUNKS):
        arrived(1, g)
        nat[g * cnat:(g + 1) * cnat, :] = unfold(rcv[1, g * crow:(g + 1) * crow, :])

    c0, c1 = col_of(comb[0:1, :]), col_of(comb[1:2, :])

    loss = jnp.zeros((rows, 1), F32)
    part0 = jnp.zeros((rows, 1), F32)
    part1 = jnp.zeros((rows, 1), F32)
    for n in range(width // 512):
        c = slice(n * 512, (n + 1) * 512)
        both = dot(sel[...], nat[:, c])
        p0, p1 = both[0:rows], both[rows:2 * rows]
        mixed = tok[:, c].astype(F32) + c0 * p0 + c1 * p1
        cotangent = mask_col * mixed
        cot[:, c] = cotangent
        loss = loss + jnp.sum(cotangent * mixed, axis=1, keepdims=True)
        part0 = part0 + jnp.sum(cotangent * p0, axis=1, keepdims=True)
        part1 = part1 + jnp.sum(cotangent * p1, axis=1, keepdims=True)
        nat[0:rows, c] = (c0 * cotangent).astype(BF16)
        nat[rows:2 * rows, c] = (c1 * cotangent).astype(BF16)

    for g in range(CHUNKS):
        a, b = place(g)
        block = dot(jnp.concatenate([a, b], axis=1), nat[...]).astype(BF16)
        snd[2, g * crow:(g + 1) * crow, :] = fold(block)
        start(2, g, 1)

    num[...] = reduce_end(4, head_n, cy, red_send, red_recv)

    @pl.when(me_c == 0)
    def _():
        pl.semaphore_wait(barrier, dp_n - 1)
        reduce_start(5, dp_n, me_z, "dp", num, cz, red_send, red_recv)

    stats[...] = jnp.zeros_like(stats)
    stats[12:13, :] = jnp.broadcast_to(jnp.sum(loss, axis=0, keepdims=True), (1, 128))

    gain_part = [jnp.zeros((1, tile), F32) for _ in range(tiles)]
    for g in range(CHUNKS):
        arrived(2, g)
        r = slice(g * cnat, (g + 1) * cnat)
        nat[0:cnat, :] = unfold(rcv[2, g * crow:(g + 1) * crow, :])

        def down_t(n, _):
            c = at(n, tile)
            hidden_grad = dot(nat[0:cnat, :], wdown_t[:, c])
            nat[cnat:2 * cnat, c] = (hidden_grad * slope[r, c]).astype(BF16)
            return _
        lax.fori_loop(0, tiles, down_t, 0)
        for n in range(tiles):
            c = slice(n * tile, (n + 1) * tile)
            row_grad = dot(nat[cnat:2 * cnat, :], wup_t[:, c]).astype(BF16)
            gain_part[n] = gain_part[n] + jnp.sum(
                row_grad.astype(F32) * xs[r, c].astype(F32), axis=0, keepdims=True)
            nat[2 * cnat:3 * cnat, c] = row_grad
        snd[3, g * crow:(g + 1) * crow, :] = fold(nat[2 * cnat:3 * cnat, :])
        if g == CHUNKS - 1:
            for n in range(tiles):
                for k in range(tile // 128):
                    at_k = n * (tile // 128) + k
                    stats[at_k:at_k + 1, :] = (
                        gain_part[n][:, k * 128:(k + 1) * 128]
                        / gain[:, at_k * 128:(at_k + 1) * 128])
            reduce_start(0, seq_n, me_s, "seq", stats, ars, red_send, red_recv)
        if g < CHUNKS - HELD:
            start(3, g, -1)

    stats[...] = reduce_end(0, seq_n, ars, red_send, red_recv)
    reduce_start(1, head_n, me_h, "head", stats, ary, red_send, red_recv)
    for g in range(CHUNKS - HELD, CHUNKS):
        start(3, g, -1)
    stats[...] = reduce_end(1, head_n, ary, red_send, red_recv)

    @pl.when(me_c == 0)
    def _():
        reduce_start(2, dp_n, me_z, "dp", stats, arz, red_send, red_recv)
        num_all[...] = reduce_end(5, dp_n, cz, red_send, red_recv)
        copy = to_mate(0, num_all, num_all)
        copy.start()
        copy.wait_send()

    @pl.when(me_c == 1)
    def _():
        to_mate(0, num_all, num_all).wait_recv()

    count = num_all[0:1, 0:1]
    ratio = (rows * dp_n * peers) / count
    out_comb[0:1, :] = ratio * as_row(part0)
    out_comb[1:2, :] = ratio * as_row(part1)
    sel[0:rows, :] = sel[0:rows, :] + sel[rows:2 * rows, :]

    for g in range(CHUNKS):
        arrived(3, g)
        nat[g * cnat:(g + 1) * cnat, :] = unfold(rcv[3, g * crow:(g + 1) * crow, :])
    for n in range(width // 512):
        c = slice(n * 512, (n + 1) * 512)
        slope[0:rows, c] = dot(sel[0:rows, :], nat[:, c])

    def last(b, _):
        r = at(b, BR)
        inverse = inv[r, :]
        normed = tok[r, :].astype(F32) * inverse
        grad = slope[r, :] * gain[...]
        mean = jnp.mean(grad * normed, axis=1, keepdims=True)
        out_tok[r, :] = (ratio * (cot[r, :] + inverse * (grad - normed * mean))).astype(BF16)
        return _
    lax.fori_loop(0, rows // BR, last, 0)

    for phase in range(4):
        sent = snd.at[phase, pl.ds(msg, (peers - 1) * msg)]
        pltpu.make_async_copy(sent, sent, send_sem.at[phase]).wait()

    @pl.when(me_c == 0)
    def _():
        stats_all[...] = reduce_end(2, dp_n, arz, red_send, red_recv)
        copy = to_mate(1, stats_all, stats_all)
        copy.start()
        copy.wait_send()

    @pl.when(me_c == 1)
    def _():
        to_mate(1, stats_all, stats_all).wait_recv()

    out_gain[...] = stats_all[0:width // 128, :] / count
    out_loss[...] = stats_all[12:13, 0:1] / (2.0 * width * count)


def reduce_start(stage, n, me, axis, stats, parts, send_sem, recv_sem):
    parts[pl.ds(n, 1)] = stats[...][None]
    parts[pl.ds(me, 1)] = stats[...][None]

    def one(j, _):
        pltpu.make_async_remote_copy(
            src_ref=parts.at[pl.ds(n, 1)], dst_ref=parts.at[pl.ds(me, 1)],
            send_sem=send_sem.at[stage], recv_sem=recv_sem.at[stage],
            device_id={axis: (me + j) % n}, device_id_type=MESH).start()
        return _
    lax.fori_loop(1, n, one, 0)


def reduce_end(stage, n, parts, send_sem, recv_sem):
    where = parts.at[pl.ds(0, n - 1)]
    pltpu.make_async_copy(where, where, recv_sem.at[stage]).wait()
    pltpu.make_async_copy(where, where, send_sem.at[stage]).wait()
    total = parts[0]
    for k in range(1, n):
        total = total + parts[k]
    return total


def solution(mesh):
    sizes = (mesh.shape["dp"], mesh.shape["seq"], mesh.shape["head"])

    def on_device(tokens, norm_gain, w_up, w_down, routes, combine, loss_mask):
        rows, width = tokens.shape
        peers = sizes[1] * sizes[2]
        slots = peers * CAP
        folded = (4, slots * FOLD, width // FOLD)
        vmem = pl.BlockSpec(memory_space=pltpu.VMEM)
        hbm = pl.BlockSpec(memory_space=pltpu.HBM)
        keep = lambda x: pltpu.with_memory_space_constraint(x, pltpu.HBM)
        grad_tokens, grad_gain, grad_combine, loss = pl.pallas_call(
            lambda *refs: kernel(sizes, *refs),
            out_shape=(
                jax.ShapeDtypeStruct((rows, width), BF16),
                jax.ShapeDtypeStruct((width // 128, 128), F32),
                jax.ShapeDtypeStruct((2, rows), F32),
                jax.ShapeDtypeStruct((1, 1), F32),
            ),
            in_specs=[hbm] * 7,
            out_specs=(vmem, vmem, vmem, vmem),
            scratch_shapes=[
                pltpu.VMEM((rows, width), BF16),
                pltpu.VMEM((width // 128, 128), F32),
                pltpu.VMEM((2, rows), I32),
                pltpu.VMEM((2, rows), F32),
                pltpu.VMEM((1, rows), I32),
                pltpu.VMEM((1, width), F32),
                pltpu.VMEM((rows, 1), F32),
                pltpu.VMEM(w_up.shape[1:], BF16),
                pltpu.VMEM(w_down.shape[1:], BF16),
                pltpu.VMEM(w_up.shape[1:], BF16),
                pltpu.VMEM(w_down.shape[1:], BF16),
                pltpu.VMEM(folded, BF16),
                pltpu.VMEM(folded, BF16),
                pltpu.VMEM((slots, width), BF16),
                pltpu.VMEM((slots, width), F32),
                pltpu.VMEM((slots, width), BF16),
                pltpu.VMEM((2 * rows, slots), BF16),
                pltpu.VMEM((rows, width), F32),
                pltpu.VMEM((16, 128), F32),
                pltpu.VMEM((sizes[0] + 1, 16, 128), F32),
                pltpu.VMEM((sizes[1] + 1, 16, 128), F32),
                pltpu.VMEM((sizes[2] + 1, 16, 128), F32),
                pltpu.VMEM((8, 128), F32),
                pltpu.VMEM((sizes[0] + 1, 8, 128), F32),
                pltpu.VMEM((sizes[1] + 1, 8, 128), F32),
                pltpu.VMEM((sizes[2] + 1, 8, 128), F32),
                pltpu.VMEM((16, 128), F32),
                pltpu.VMEM((8, 128), F32),
                pltpu.SemaphoreType.DMA((4,)),
                pltpu.SemaphoreType.DMA((4, CHUNKS)),
                pltpu.SemaphoreType.DMA((8,)),
                pltpu.SemaphoreType.DMA((6,)),
                pltpu.SemaphoreType.DMA((6,)),
                pltpu.SemaphoreType.REGULAR,
                pltpu.SemaphoreType.DMA((2,)),
                pltpu.SemaphoreType.DMA((2,)),
            ],
            compiler_params=pltpu.CompilerParams(
                collective_id=1, has_side_effects=True, vmem_limit_bytes=48 * 2**20),
            cost_estimate=pl.CostEstimate(
                flops=8 * slots * width * width, bytes_accessed=4 * width * width,
                transcendentals=slots * width),
            name="moe",
        )(*map(keep, (tokens, norm_gain.reshape(width // 128, 128), w_up, w_down, routes.T,
                      combine.T, loss_mask.reshape(1, rows))))
        return grad_tokens, grad_gain.reshape(width), grad_combine.T, loss.reshape(())

    split = ("dp", "seq", "head")
    in_specs = (P(split, None), P(), P(("seq", "head"), None, None), P(("seq", "head"), None, None),
                P(split, None), P(split, None), P(split))
    out_specs = (P(split, None), P(), P(split, None), P())
    return jax.shard_map(on_device, mesh=mesh, in_specs=in_specs, out_specs=out_specs,
                         check_vma=False)
```

```python
import jax
import jax.numpy as jnp
from jax import lax
from jax.experimental import pallas as pl
from jax.experimental.pallas import tpu as pltpu
from jax.sharding import PartitionSpec as P

F32, BF16, I32 = jnp.float32, jnp.bfloat16, jnp.int32
MESH = pl.DeviceIdType.MESH
CAP = 4
FOLD = 4
CHUNKS = 4


def dot(a, b):
    return jnp.dot(a, b, preferred_element_type=F32)


def iota(shape, dim):
    return lax.broadcasted_iota(I32, shape, dim)


def kernel(sizes, tok_hbm, gain_hbm, wup_hbm, wdown_hbm, routes_hbm, comb_hbm, mask_hbm,
           out_tok, out_gain, out_comb, out_loss,
           tok, gain_v, routes, comb, mask, gain, inv,
           wup, wdown, wup_t, wdown_t, snd, rcv, xs, slope, nat, sel, cot, stats, arz, ars, ary, num, cz, cs, cy,
           stats_all, num_all,
           send_sem, recv_sem, w_sem, red_send, red_recv, go, mate_send, mate_recv):
    dp_n, seq_n, head_n = sizes
    rows, width = tok.shape
    peers = seq_n * head_n
    per = peers // CHUNKS
    msg = CAP * FOLD
    crow = per * msg
    cnat = per * CAP
    cols = width // FOLD
    slots = peers * CAP
    xn = seq_n // 2
    me_z = lax.axis_index("dp")
    me_s = lax.axis_index("seq")
    me_h = lax.axis_index("head")
    me_x, me_c = me_s // 2, me_s % 2

    def at_offset(g, i, sign):
        dc, dh = i % 2, i // 2
        dx = (g + dh) % xn
        x = (me_x + sign * dx + xn) % xn
        return {"seq": x * 2 + (me_c + dc) % 2, "head": (me_h + sign * dh + head_n) % head_n}

    pairs = ((routes_hbm, routes), (mask_hbm, mask), (comb_hbm, comb), (gain_hbm, gain_v),
             (tok_hbm, tok), (wup_hbm.at[0], wup), (wdown_hbm.at[0], wdown))
    loads = [pltpu.make_async_copy(a, b, w_sem.at[i]) for i, (a, b) in enumerate(pairs)]
    for load in loads:
        load.start()

    barrier = pltpu.get_barrier_semaphore()

    def greet(j, _):
        x, h = (me_x + j // head_n) % xn, (me_h + j % head_n) % head_n
        pl.semaphore_signal(barrier, inc=1, device_id={"seq": x * 2 + 1, "head": h},
                            device_id_type=MESH)
        return _
    lax.fori_loop(me_c, peers // 2, greet, 0)
    mate = {"seq": me_x * 2 + 1 - me_c}

    def plane_ready():
        @pl.when(me_c == 1)
        def _():
            pl.semaphore_wait(barrier, peers - 1)
            pl.semaphore_signal(go, inc=1, device_id=mate, device_id_type=MESH)

        @pl.when(me_c == 0)
        def _():
            pl.semaphore_wait(go, 1)

    def to_mate(i, src, dst):
        return pltpu.make_async_remote_copy(src_ref=src, dst_ref=dst, send_sem=mate_send.at[i],
                                            recv_sem=mate_recv.at[i], device_id=mate,
                                            device_id_type=MESH)

    q, m = iota((crow, crow), 0), iota((crow, crow), 1)
    fold_m = (m == ((q // CAP) % FOLD) * cnat + (q // msg) * CAP + q % CAP).astype(BF16)
    back_m = (q == ((m // CAP) % FOLD) * cnat + (m // msg) * CAP + m % CAP).astype(BF16)

    def fold(block):
        stack = jnp.concatenate([block[:, c * cols:(c + 1) * cols] for c in range(FOLD)], axis=0)
        return dot(fold_m, stack).astype(BF16)

    def unfold(block):
        stack = dot(back_m, block).astype(BF16)
        return jnp.concatenate([stack[c * cnat:(c + 1) * cnat] for c in range(FOLD)], axis=1)

    def at(g, n):
        return pl.ds(pl.multiple_of(g * n, n), n)

    def start(phase, g, sign):
        def one(i, _):
            where = at(g * per + i, msg)
            pltpu.make_async_remote_copy(
                src_ref=snd.at[phase, where], dst_ref=rcv.at[phase, where],
                send_sem=send_sem.at[phase], recv_sem=recv_sem.at[phase, g],
                device_id=at_offset(g, i, sign), device_id_type=MESH).start()
            return _
        lax.fori_loop(1 if g == 0 else 0, per, one, 0)
        if g == 0:
            pltpu.make_async_copy(snd.at[phase, pl.ds(0, msg)], rcv.at[phase, pl.ds(0, msg)],
                                  recv_sem.at[phase, 0]).start()

    def arrived(phase, g):
        where = rcv.at[phase, at(g, crow)]
        pltpu.make_async_copy(where, where, recv_sem.at[phase, g]).wait()

    BR = 32

    for load in loads[:3]:
        load.wait()
    eye = iota((rows, rows), 0) == iota((rows, rows), 1)
    earlier = (iota((rows, rows), 0) < iota((rows, rows), 1)).astype(BF16)
    r0, r1 = routes[0:1, :], routes[1:2, :]
    experts = iota((peers, rows), 0)
    hot0, hot1 = (experts == r0).astype(F32), (experts == r1).astype(F32)
    before = dot((hot0 + hot1).astype(BF16), earlier)

    def slot_of(r, hot):
        turn = jnp.sum(before * hot, axis=0, keepdims=True).astype(I32)
        s, h = r // head_n, r % head_n
        dx = (s // 2 - me_x + xn) % xn
        dc = (s % 2 + me_c) % 2
        dh = (h - me_h + head_n) % head_n
        g = (dx - dh + head_n) % xn
        return (g * per + dh * 2 + dc) * CAP + turn

    def col_of(row):
        return jnp.sum(jnp.where(eye, row.astype(F32), 0.0), axis=1, keepdims=True)

    def as_row(col):
        return jnp.sum(jnp.where(eye, col, 0.0), axis=0, keepdims=True)

    s0_row, s1_row = slot_of(r0, hot0), slot_of(r1, hot1)
    s0, s1 = col_of(s0_row).astype(I32), col_of(s1_row).astype(I32)
    mask_col = col_of(mask[...])

    for load in loads[3:5]:
        load.wait()
    for k in range(width // 128):
        gain[:, k * 128:(k + 1) * 128] = gain_v[k:k + 1, :]

    def norm(b, _):
        r = at(b, BR)
        x = tok[r, :].astype(F32)
        inverse = lax.rsqrt(jnp.mean(x * x, axis=1, keepdims=True) + 1e-05)
        inv[r, :] = inverse
        nat[r, :] = (x * inverse * gain[...]).astype(BF16)
        return _
    lax.fori_loop(0, rows // BR, norm, 0)

    slot_lanes = iota((rows, slots), 1)
    pick0 = (slot_lanes == s0).astype(BF16)
    pick1 = (slot_lanes == s1).astype(BF16)
    sel[0:rows, :] = pick0
    sel[rows:2 * rows, :] = pick1

    def place(g):
        target = iota((cnat, rows), 0) + g * cnat
        return (target == s0_row).astype(BF16), (target == s1_row).astype(BF16)

    for g in range(CHUNKS):
        a, b = place(g)
        block = dot(a + b, nat[0:rows, :]).astype(BF16)
        snd[0, g * crow:(g + 1) * crow, :] = fold(block)
        if g == 0:
            plane_ready()
        start(0, g, 1)

    @pl.when(me_c == 0)
    def _():
        def greet_z(j, _):
            pl.semaphore_signal(barrier, inc=1, device_id={"dp": (me_z + j) % dp_n},
                                device_id_type=MESH)
            return _
        lax.fori_loop(1, dp_n, greet_z, 0)

    num[...] = jnp.broadcast_to(jnp.sum(mask_col, axis=0, keepdims=True), (8, 128))
    reduce_start(3, seq_n, me_s, "seq", num, cs, red_send, red_recv)
    for load in loads[5:]:
        load.wait()
    tile = 768
    tiles = width // tile
    edge = 256
    blocks = width // edge

    def turn(i, _):
        a, b = at(i // blocks, edge), at(i % blocks, edge)
        wdown_t[b, a] = wdown[a, b].T
        wup_t[b, a] = wup[a, b].T
        return _
    lax.fori_loop(0, blocks * blocks, turn, 0)

    for g in range(CHUNKS):
        arrived(0, g)
        r = slice(g * cnat, (g + 1) * cnat)
        xs[r, :] = unfold(rcv[0, g * crow:(g + 1) * crow, :])

        def up(n, _):
            c = at(n, tile)
            projected = dot(xs[r, :], wup[:, c])
            gate = jax.nn.sigmoid(1.702 * projected)
            slope[r, c] = gate + 1.702 * projected * gate * (1.0 - gate)
            nat[0:cnat, c] = (projected * gate).astype(BF16)
            return _
        lax.fori_loop(0, tiles, up, 0)

        def down(n, _):
            c = at(n, tile)
            nat[cnat:2 * cnat, c] = dot(nat[0:cnat, :], wdown[:, c]).astype(BF16)
            return _
        lax.fori_loop(0, tiles, down, 0)
        snd[1, g * crow:(g + 1) * crow, :] = fold(nat[cnat:2 * cnat, :])
        start(1, g, -1)

    num[...] = reduce_end(3, seq_n, cs, red_send, red_recv)
    reduce_start(4, head_n, me_h, "head", num, cy, red_send, red_recv)

    for g in range(CHUNKS):
        arrived(1, g)
        nat[g * cnat:(g + 1) * cnat, :] = unfold(rcv[1, g * crow:(g + 1) * crow, :])

    c0, c1 = col_of(comb[0:1, :]), col_of(comb[1:2, :])

    loss = jnp.zeros((rows, 1), F32)
    part0 = jnp.zeros((rows, 1), F32)
    part1 = jnp.zeros((rows, 1), F32)
    for n in range(width // 512):
        c = slice(n * 512, (n + 1) * 512)
        both = dot(sel[...], nat[:, c])
        p0, p1 = both[0:rows], both[rows:2 * rows]
        mixed = tok[:, c].astype(F32) + c0 * p0 + c1 * p1
        cotangent = mask_col * mixed
        cot[:, c] = cotangent
        loss = loss + jnp.sum(cotangent * mixed, axis=1, keepdims=True)
        part0 = part0 + jnp.sum(cotangent * p0, axis=1, keepdims=True)
        part1 = part1 + jnp.sum(cotangent * p1, axis=1, keepdims=True)
        nat[0:rows, c] = (c0 * cotangent).astype(BF16)
        nat[rows:2 * rows, c] = (c1 * cotangent).astype(BF16)

    for g in range(CHUNKS):
        a, b = place(g)
        block = dot(jnp.concatenate([a, b], axis=1), nat[...]).astype(BF16)
        snd[2, g * crow:(g + 1) * crow, :] = fold(block)
        start(2, g, 1)

    num[...] = reduce_end(4, head_n, cy, red_send, red_recv)

    @pl.when(me_c == 0)
    def _():
        pl.semaphore_wait(barrier, dp_n - 1)
        reduce_start(5, dp_n, me_z, "dp", num, cz, red_send, red_recv)

    stats[...] = jnp.zeros_like(stats)
    stats[12:13, :] = jnp.broadcast_to(jnp.sum(loss, axis=0, keepdims=True), (1, 128))

    gain_part = [jnp.zeros((1, tile), F32) for _ in range(tiles)]
    for g in range(CHUNKS):
        arrived(2, g)
        r = slice(g * cnat, (g + 1) * cnat)
        nat[0:cnat, :] = unfold(rcv[2, g * crow:(g + 1) * crow, :])

        def down_t(n, _):
            c = at(n, tile)
            hidden_grad = dot(nat[0:cnat, :], wdown_t[:, c])
            nat[cnat:2 * cnat, c] = (hidden_grad * slope[r, c]).astype(BF16)
            return _
        lax.fori_loop(0, tiles, down_t, 0)
        for n in range(tiles):
            c = slice(n * tile, (n + 1) * tile)
            row_grad = dot(nat[cnat:2 * cnat, :], wup_t[:, c]).astype(BF16)
            gain_part[n] = gain_part[n] + jnp.sum(
                row_grad.astype(F32) * xs[r, c].astype(F32), axis=0, keepdims=True)
            nat[2 * cnat:3 * cnat, c] = row_grad
        if g == CHUNKS - 1:
            for n in range(tiles):
                for k in range(tile // 128):
                    at_k = n * (tile // 128) + k
                    stats[at_k:at_k + 1, :] = (
                        gain_part[n][:, k * 128:(k + 1) * 128]
                        / gain[:, at_k * 128:(at_k + 1) * 128])
            reduce_start(0, seq_n, me_s, "seq", stats, ars, red_send, red_recv)
            start(3, g - 1, -1)
        snd[3, g * crow:(g + 1) * crow, :] = fold(nat[2 * cnat:3 * cnat, :])
        if g < CHUNKS - 2:
            start(3, g, -1)

    stats[...] = reduce_end(0, seq_n, ars, red_send, red_recv)
    reduce_start(1, head_n, me_h, "head", stats, ary, red_send, red_recv)
    start(3, CHUNKS - 1, -1)
    stats[...] = reduce_end(1, head_n, ary, red_send, red_recv)

    @pl.when(me_c == 0)
    def _():
        reduce_start(2, dp_n, me_z, "dp", stats, arz, red_send, red_recv)
        num_all[...] = reduce_end(5, dp_n, cz, red_send, red_recv)
        copy = to_mate(0, num_all, num_all)
        copy.start()
        copy.wait_send()

    @pl.when(me_c == 1)
    def _():
        to_mate(0, num_all, num_all).wait_recv()

    count = num_all[0:1, 0:1]
    ratio = (rows * dp_n * peers) / count
    out_comb[0:1, :] = ratio * as_row(part0)
    out_comb[1:2, :] = ratio * as_row(part1)
    sel[0:rows, :] = sel[0:rows, :] + sel[rows:2 * rows, :]

    for g in range(CHUNKS):
        arrived(3, g)
        nat[g * cnat:(g + 1) * cnat, :] = unfold(rcv[3, g * crow:(g + 1) * crow, :])
    for n in range(width // 512):
        c = slice(n * 512, (n + 1) * 512)
        slope[0:rows, c] = dot(sel[0:rows, :], nat[:, c])

    def last(b, _):
        r = at(b, BR)
        inverse = inv[r, :]
        normed = tok[r, :].astype(F32) * inverse
        grad = slope[r, :] * gain[...]
        mean = jnp.mean(grad * normed, axis=1, keepdims=True)
        out_tok[r, :] = (ratio * (cot[r, :] + inverse * (grad - normed * mean))).astype(BF16)
        return _
    lax.fori_loop(0, rows // BR, last, 0)

    for phase in range(4):
        sent = snd.at[phase, pl.ds(msg, (peers - 1) * msg)]
        pltpu.make_async_copy(sent, sent, send_sem.at[phase]).wait()

    @pl.when(me_c == 0)
    def _():
        stats_all[...] = reduce_end(2, dp_n, arz, red_send, red_recv)
        copy = to_mate(1, stats_all, stats_all)
        copy.start()
        copy.wait_send()

    @pl.when(me_c == 1)
    def _():
        to_mate(1, stats_all, stats_all).wait_recv()

    out_gain[...] = stats_all[0:width // 128, :] / count
    out_loss[...] = stats_all[12:13, 0:1] / (2.0 * width * count)


def reduce_start(stage, n, me, axis, stats, parts, send_sem, recv_sem):
    parts[pl.ds(n, 1)] = stats[...][None]
    parts[pl.ds(me, 1)] = stats[...][None]

    def one(j, _):
        pltpu.make_async_remote_copy(
            src_ref=parts.at[pl.ds(n, 1)], dst_ref=parts.at[pl.ds(me, 1)],
            send_sem=send_sem.at[stage], recv_sem=recv_sem.at[stage],
            device_id={axis: (me + j) % n}, device_id_type=MESH).start()
        return _
    lax.fori_loop(1, n, one, 0)


def reduce_end(stage, n, parts, send_sem, recv_sem):
    where = parts.at[pl.ds(0, n - 1)]
    pltpu.make_async_copy(where, where, recv_sem.at[stage]).wait()
    pltpu.make_async_copy(where, where, send_sem.at[stage]).wait()
    total = parts[0]
    for k in range(1, n):
        total = total + parts[k]
    return total


def solution(mesh):
    sizes = (mesh.shape["dp"], mesh.shape["seq"], mesh.shape["head"])

    def on_device(tokens, norm_gain, w_up, w_down, routes, combine, loss_mask):
        rows, width = tokens.shape
        peers = sizes[1] * sizes[2]
        slots = peers * CAP
        folded = (4, slots * FOLD, width // FOLD)
        vmem = pl.BlockSpec(memory_space=pltpu.VMEM)
        hbm = pl.BlockSpec(memory_space=pltpu.HBM)
        keep = lambda x: pltpu.with_memory_space_constraint(x, pltpu.HBM)
        grad_tokens, grad_gain, grad_combine, loss = pl.pallas_call(
            lambda *refs: kernel(sizes, *refs),
            out_shape=(
                jax.ShapeDtypeStruct((rows, width), BF16),
                jax.ShapeDtypeStruct((width // 128, 128), F32),
                jax.ShapeDtypeStruct((2, rows), F32),
                jax.ShapeDtypeStruct((1, 1), F32),
            ),
            in_specs=[hbm] * 7,
            out_specs=(vmem, vmem, vmem, vmem),
            scratch_shapes=[
                pltpu.VMEM((rows, width), BF16),
                pltpu.VMEM((width // 128, 128), F32),
                pltpu.VMEM((2, rows), I32),
                pltpu.VMEM((2, rows), F32),
                pltpu.VMEM((1, rows), I32),
                pltpu.VMEM((1, width), F32),
                pltpu.VMEM((rows, 1), F32),
                pltpu.VMEM(w_up.shape[1:], BF16),
                pltpu.VMEM(w_down.shape[1:], BF16),
                pltpu.VMEM(w_up.shape[1:], BF16),
                pltpu.VMEM(w_down.shape[1:], BF16),
                pltpu.VMEM(folded, BF16),
                pltpu.VMEM(folded, BF16),
                pltpu.VMEM((slots, width), BF16),
                pltpu.VMEM((slots, width), F32),
                pltpu.VMEM((slots, width), BF16),
                pltpu.VMEM((2 * rows, slots), BF16),
                pltpu.VMEM((rows, width), F32),
                pltpu.VMEM((16, 128), F32),
                pltpu.VMEM((sizes[0] + 1, 16, 128), F32),
                pltpu.VMEM((sizes[1] + 1, 16, 128), F32),
                pltpu.VMEM((sizes[2] + 1, 16, 128), F32),
                pltpu.VMEM((8, 128), F32),
                pltpu.VMEM((sizes[0] + 1, 8, 128), F32),
                pltpu.VMEM((sizes[1] + 1, 8, 128), F32),
                pltpu.VMEM((sizes[2] + 1, 8, 128), F32),
                pltpu.VMEM((16, 128), F32),
                pltpu.VMEM((8, 128), F32),
                pltpu.SemaphoreType.DMA((4,)),
                pltpu.SemaphoreType.DMA((4, CHUNKS)),
                pltpu.SemaphoreType.DMA((8,)),
                pltpu.SemaphoreType.DMA((6,)),
                pltpu.SemaphoreType.DMA((6,)),
                pltpu.SemaphoreType.REGULAR,
                pltpu.SemaphoreType.DMA((2,)),
                pltpu.SemaphoreType.DMA((2,)),
            ],
            compiler_params=pltpu.CompilerParams(
                collective_id=1, has_side_effects=True, vmem_limit_bytes=48 * 2**20),
            cost_estimate=pl.CostEstimate(
                flops=8 * slots * width * width, bytes_accessed=4 * width * width,
                transcendentals=slots * width),
            name="moe",
        )(*map(keep, (tokens, norm_gain.reshape(width // 128, 128), w_up, w_down, routes.T,
                      combine.T, loss_mask.reshape(1, rows))))
        return grad_tokens, grad_gain.reshape(width), grad_combine.T, loss.reshape(())

    split = ("dp", "seq", "head")
    in_specs = (P(split, None), P(), P(("seq", "head"), None, None), P(("seq", "head"), None, None),
                P(split, None), P(split, None), P(split))
    out_specs = (P(split, None), P(), P(split, None), P())
    return jax.shard_map(on_device, mesh=mesh, in_specs=in_specs, out_specs=out_specs,
                         check_vma=False)
```

```python
import jax
import jax.numpy as jnp
from jax import lax
from jax.experimental import pallas as pl
from jax.experimental.pallas import tpu as pltpu
from jax.sharding import PartitionSpec as P

F32, BF16, I32 = jnp.float32, jnp.bfloat16, jnp.int32
MESH = pl.DeviceIdType.MESH
CAP = 4
FOLD = 4
CHUNKS = 4
HELD = 2


def dot(a, b):
    return jnp.dot(a, b, preferred_element_type=F32)


def iota(shape, dim):
    return lax.broadcasted_iota(I32, shape, dim)


def kernel(sizes, tok_hbm, gain_hbm, wup_hbm, wdown_hbm, routes_hbm, comb_hbm, mask_hbm,
           out_tok, out_gain, out_comb, out_loss,
           tok, gain_v, routes, comb, mask, gain, inv,
           wup, wdown, wup_t, wdown_t, snd, rcv, xs, slope, nat, sel, cot, stats, arz, ars, ary, num, cz, cs, cy,
           stats_all, num_all,
           send_sem, recv_sem, w_sem, red_send, red_recv, go, mate_send, mate_recv):
    dp_n, seq_n, head_n = sizes
    rows, width = tok.shape
    peers = seq_n * head_n
    per = peers // CHUNKS
    msg = CAP * FOLD
    crow = per * msg
    cnat = per * CAP
    cols = width // FOLD
    slots = peers * CAP
    xn = seq_n // 2
    me_z = lax.axis_index("dp")
    me_s = lax.axis_index("seq")
    me_h = lax.axis_index("head")
    me_x, me_c = me_s // 2, me_s % 2

    def at_offset(g, i, sign):
        dc, dh = i % 2, i // 2
        dx = (g + dh) % xn
        x = (me_x + sign * dx + xn) % xn
        return {"seq": x * 2 + (me_c + dc) % 2, "head": (me_h + sign * dh + head_n) % head_n}

    pairs = ((routes_hbm, routes), (mask_hbm, mask), (comb_hbm, comb), (gain_hbm, gain_v),
             (tok_hbm, tok), (wup_hbm.at[0], wup), (wdown_hbm.at[0], wdown))
    loads = [pltpu.make_async_copy(a, b, w_sem.at[i]) for i, (a, b) in enumerate(pairs)]
    for load in loads:
        load.start()

    barrier = pltpu.get_barrier_semaphore()

    def greet(j, _):
        x, h = (me_x + j // head_n) % xn, (me_h + j % head_n) % head_n
        pl.semaphore_signal(barrier, inc=1, device_id={"seq": x * 2 + 1, "head": h},
                            device_id_type=MESH)
        return _
    lax.fori_loop(me_c, peers // 2, greet, 0)
    mate = {"seq": me_x * 2 + 1 - me_c}

    def plane_ready():
        @pl.when(me_c == 1)
        def _():
            pl.semaphore_wait(barrier, peers - 1)
            pl.semaphore_signal(go, inc=1, device_id=mate, device_id_type=MESH)

        @pl.when(me_c == 0)
        def _():
            pl.semaphore_wait(go, 1)

    def to_mate(i, src, dst):
        return pltpu.make_async_remote_copy(src_ref=src, dst_ref=dst, send_sem=mate_send.at[i],
                                            recv_sem=mate_recv.at[i], device_id=mate,
                                            device_id_type=MESH)

    q, m = iota((crow, crow), 0), iota((crow, crow), 1)
    fold_m = (m == ((q // CAP) % FOLD) * cnat + (q // msg) * CAP + q % CAP).astype(BF16)
    back_m = (q == ((m // CAP) % FOLD) * cnat + (m // msg) * CAP + m % CAP).astype(BF16)

    def fold(block):
        stack = jnp.concatenate([block[:, c * cols:(c + 1) * cols] for c in range(FOLD)], axis=0)
        return dot(fold_m, stack).astype(BF16)

    def unfold(block):
        stack = dot(back_m, block).astype(BF16)
        return jnp.concatenate([stack[c * cnat:(c + 1) * cnat] for c in range(FOLD)], axis=1)

    def at(g, n):
        return pl.ds(pl.multiple_of(g * n, n), n)

    def start(phase, g, sign):
        def one(i, _):
            where = at(g * per + i, msg)
            pltpu.make_async_remote_copy(
                src_ref=snd.at[phase, where], dst_ref=rcv.at[phase, where],
                send_sem=send_sem.at[phase], recv_sem=recv_sem.at[phase, g],
                device_id=at_offset(g, i, sign), device_id_type=MESH).start()
            return _
        lax.fori_loop(1 if g == 0 else 0, per, one, 0)
        if g == 0:
            pltpu.make_async_copy(snd.at[phase, pl.ds(0, msg)], rcv.at[phase, pl.ds(0, msg)],
                                  recv_sem.at[phase, 0]).start()

    def arrived(phase, g):
        where = rcv.at[phase, at(g, crow)]
        pltpu.make_async_copy(where, where, recv_sem.at[phase, g]).wait()

    BR = 32

    for load in loads[:3]:
        load.wait()
    eye = iota((rows, rows), 0) == iota((rows, rows), 1)
    earlier = (iota((rows, rows), 0) < iota((rows, rows), 1)).astype(BF16)
    r0, r1 = routes[0:1, :], routes[1:2, :]
    experts = iota((peers, rows), 0)
    hot0, hot1 = (experts == r0).astype(F32), (experts == r1).astype(F32)
    before = dot((hot0 + hot1).astype(BF16), earlier)

    def slot_of(r, hot):
        turn = jnp.sum(before * hot, axis=0, keepdims=True).astype(I32)
        s, h = r // head_n, r % head_n
        dx = (s // 2 - me_x + xn) % xn
        dc = (s % 2 + me_c) % 2
        dh = (h - me_h + head_n) % head_n
        g = (dx - dh + head_n) % xn
        return (g * per + dh * 2 + dc) * CAP + turn

    def col_of(row):
        return jnp.sum(jnp.where(eye, row.astype(F32), 0.0), axis=1, keepdims=True)

    def as_row(col):
        return jnp.sum(jnp.where(eye, col, 0.0), axis=0, keepdims=True)

    s0_row, s1_row = slot_of(r0, hot0), slot_of(r1, hot1)
    s0, s1 = col_of(s0_row).astype(I32), col_of(s1_row).astype(I32)
    mask_col = col_of(mask[...])

    for load in loads[3:5]:
        load.wait()
    for k in range(width // 128):
        gain[:, k * 128:(k + 1) * 128] = gain_v[k:k + 1, :]

    def norm(b, _):
        r = at(b, BR)
        x = tok[r, :].astype(F32)
        inverse = lax.rsqrt(jnp.mean(x * x, axis=1, keepdims=True) + 1e-05)
        inv[r, :] = inverse
        nat[r, :] = (x * inverse * gain[...]).astype(BF16)
        return _
    lax.fori_loop(0, rows // BR, norm, 0)

    slot_lanes = iota((rows, slots), 1)
    pick0 = (slot_lanes == s0).astype(BF16)
    pick1 = (slot_lanes == s1).astype(BF16)
    sel[0:rows, :] = pick0
    sel[rows:2 * rows, :] = pick1

    def place(g):
        target = iota((cnat, rows), 0) + g * cnat
        return (target == s0_row).astype(BF16), (target == s1_row).astype(BF16)

    for g in range(CHUNKS):
        a, b = place(g)
        block = dot(a + b, nat[0:rows, :]).astype(BF16)
        snd[0, g * crow:(g + 1) * crow, :] = fold(block)
        if g == 0:
            plane_ready()
        start(0, g, 1)

    @pl.when(me_c == 0)
    def _():
        def greet_z(j, _):
            pl.semaphore_signal(barrier, inc=1, device_id={"dp": (me_z + j) % dp_n},
                                device_id_type=MESH)
            return _
        lax.fori_loop(1, dp_n, greet_z, 0)

    num[...] = jnp.broadcast_to(jnp.sum(mask_col, axis=0, keepdims=True), (8, 128))
    reduce_start(3, seq_n, me_s, "seq", num, cs, red_send, red_recv)
    for load in loads[5:]:
        load.wait()
    tile = 768
    tiles = width // tile
    edge = 256
    blocks = width // edge

    def turn(i, _):
        a, b = at(i // blocks, edge), at(i % blocks, edge)
        wdown_t[b, a] = wdown[a, b].T
        wup_t[b, a] = wup[a, b].T
        return _
    lax.fori_loop(0, blocks * blocks, turn, 0)

    for g in range(CHUNKS):
        arrived(0, g)
        r = slice(g * cnat, (g + 1) * cnat)
        xs[r, :] = unfold(rcv[0, g * crow:(g + 1) * crow, :])

        def up(n, _):
            c = at(n, tile)
            projected = dot(xs[r, :], wup[:, c])
            gate = jax.nn.sigmoid(1.702 * projected)
            slope[r, c] = gate + 1.702 * projected * gate * (1.0 - gate)
            nat[0:cnat, c] = (projected * gate).astype(BF16)
            return _
        lax.fori_loop(0, tiles, up, 0)

        def down(n, _):
            c = at(n, tile)
            nat[cnat:2 * cnat, c] = dot(nat[0:cnat, :], wdown[:, c]).astype(BF16)
            return _
        lax.fori_loop(0, tiles, down, 0)
        snd[1, g * crow:(g + 1) * crow, :] = fold(nat[cnat:2 * cnat, :])
        start(1, g, -1)

    num[...] = reduce_end(3, seq_n, cs, red_send, red_recv)
    reduce_start(4, head_n, me_h, "head", num, cy, red_send, red_recv)

    for g in range(CHUNKS):
        arrived(1, g)
        nat[g * cnat:(g + 1) * cnat, :] = unfold(rcv[1, g * crow:(g + 1) * crow, :])

    c0, c1 = col_of(comb[0:1, :]), col_of(comb[1:2, :])

    loss = jnp.zeros((rows, 1), F32)
    part0 = jnp.zeros((rows, 1), F32)
    part1 = jnp.zeros((rows, 1), F32)
    for n in range(width // 512):
        c = slice(n * 512, (n + 1) * 512)
        both = dot(sel[...], nat[:, c])
        p0, p1 = both[0:rows], both[rows:2 * rows]
        mixed = tok[:, c].astype(F32) + c0 * p0 + c1 * p1
        cotangent = mask_col * mixed
        cot[:, c] = cotangent
        loss = loss + jnp.sum(cotangent * mixed, axis=1, keepdims=True)
        part0 = part0 + jnp.sum(cotangent * p0, axis=1, keepdims=True)
        part1 = part1 + jnp.sum(cotangent * p1, axis=1, keepdims=True)
        nat[0:rows, c] = (c0 * cotangent).astype(BF16)
        nat[rows:2 * rows, c] = (c1 * cotangent).astype(BF16)

    for g in range(CHUNKS):
        a, b = place(g)
        block = dot(jnp.concatenate([a, b], axis=1), nat[...]).astype(BF16)
        snd[2, g * crow:(g + 1) * crow, :] = fold(block)
        start(2, g, 1)

    num[...] = reduce_end(4, head_n, cy, red_send, red_recv)

    @pl.when(me_c == 0)
    def _():
        pl.semaphore_wait(barrier, dp_n - 1)
        reduce_start(5, dp_n, me_z, "dp", num, cz, red_send, red_recv)

    stats[...] = jnp.zeros_like(stats)
    stats[12:13, :] = jnp.broadcast_to(jnp.sum(loss, axis=0, keepdims=True), (1, 128))

    gain_part = [jnp.zeros((1, tile), F32) for _ in range(tiles)]
    for g in range(CHUNKS):
        arrived(2, g)
        r = slice(g * cnat, (g + 1) * cnat)
        nat[0:cnat, :] = unfold(rcv[2, g * crow:(g + 1) * crow, :])

        def down_t(n, _):
            c = at(n, tile)
            hidden_grad = dot(nat[0:cnat, :], wdown_t[:, c])
            nat[cnat:2 * cnat, c] = (hidden_grad * slope[r, c]).astype(BF16)
            return _
        lax.fori_loop(0, tiles, down_t, 0)
        for n in range(tiles):
            c = slice(n * tile, (n + 1) * tile)
            row_grad = dot(nat[cnat:2 * cnat, :], wup_t[:, c]).astype(BF16)
            gain_part[n] = gain_part[n] + jnp.sum(
                row_grad.astype(F32) * xs[r, c].astype(F32), axis=0, keepdims=True)
            nat[2 * cnat:3 * cnat, c] = row_grad
        if g == CHUNKS - 1:
            for n in range(tiles):
                for k in range(tile // 128):
                    at_k = n * (tile // 128) + k
                    stats[at_k:at_k + 1, :] = (
                        gain_part[n][:, k * 128:(k + 1) * 128]
                        / gain[:, at_k * 128:(at_k + 1) * 128])
            reduce_start(0, seq_n, me_s, "seq", stats, ars, red_send, red_recv)
        snd[3, g * crow:(g + 1) * crow, :] = fold(nat[2 * cnat:3 * cnat, :])
        if g < CHUNKS - HELD:
            start(3, g, -1)

    stats[...] = reduce_end(0, seq_n, ars, red_send, red_recv)
    reduce_start(1, head_n, me_h, "head", stats, ary, red_send, red_recv)
    for g in range(CHUNKS - HELD, CHUNKS):
        start(3, g, -1)
    stats[...] = reduce_end(1, head_n, ary, red_send, red_recv)

    @pl.when(me_c == 0)
    def _():
        reduce_start(2, dp_n, me_z, "dp", stats, arz, red_send, red_recv)
        num_all[...] = reduce_end(5, dp_n, cz, red_send, red_recv)
        copy = to_mate(0, num_all, num_all)
        copy.start()
        copy.wait_send()

    @pl.when(me_c == 1)
    def _():
        to_mate(0, num_all, num_all).wait_recv()

    count = num_all[0:1, 0:1]
    ratio = (rows * dp_n * peers) / count
    out_comb[0:1, :] = ratio * as_row(part0)
    out_comb[1:2, :] = ratio * as_row(part1)
    sel[0:rows, :] = sel[0:rows, :] + sel[rows:2 * rows, :]

    for g in range(CHUNKS):
        arrived(3, g)
        nat[g * cnat:(g + 1) * cnat, :] = unfold(rcv[3, g * crow:(g + 1) * crow, :])
    for n in range(width // 512):
        c = slice(n * 512, (n + 1) * 512)
        slope[0:rows, c] = dot(sel[0:rows, :], nat[:, c])

    def last(b, _):
        r = at(b, BR)
        inverse = inv[r, :]
        normed = tok[r, :].astype(F32) * inverse
        grad = slope[r, :] * gain[...]
        mean = jnp.mean(grad * normed, axis=1, keepdims=True)
        out_tok[r, :] = (ratio * (cot[r, :] + inverse * (grad - normed * mean))).astype(BF16)
        return _
    lax.fori_loop(0, rows // BR, last, 0)

    for phase in range(4):
        sent = snd.at[phase, pl.ds(msg, (peers - 1) * msg)]
        pltpu.make_async_copy(sent, sent, send_sem.at[phase]).wait()

    @pl.when(me_c == 0)
    def _():
        stats_all[...] = reduce_end(2, dp_n, arz, red_send, red_recv)
        copy = to_mate(1, stats_all, stats_all)
        copy.start()
        copy.wait_send()

    @pl.when(me_c == 1)
    def _():
        to_mate(1, stats_all, stats_all).wait_recv()

    out_gain[...] = stats_all[0:width // 128, :] / count
    out_loss[...] = stats_all[12:13, 0:1] / (2.0 * width * count)


def reduce_start(stage, n, me, axis, stats, parts, send_sem, recv_sem):
    parts[pl.ds(n, 1)] = stats[...][None]
    parts[pl.ds(me, 1)] = stats[...][None]

    def one(j, _):
        pltpu.make_async_remote_copy(
            src_ref=parts.at[pl.ds(n, 1)], dst_ref=parts.at[pl.ds(me, 1)],
            send_sem=send_sem.at[stage], recv_sem=recv_sem.at[stage],
            device_id={axis: (me + j) % n}, device_id_type=MESH).start()
        return _
    lax.fori_loop(1, n, one, 0)


def reduce_end(stage, n, parts, send_sem, recv_sem):
    where = parts.at[pl.ds(0, n - 1)]
    pltpu.make_async_copy(where, where, recv_sem.at[stage]).wait()
    pltpu.make_async_copy(where, where, send_sem.at[stage]).wait()
    total = parts[0]
    for k in range(1, n):
        total = total + parts[k]
    return total


def solution(mesh):
    sizes = (mesh.shape["dp"], mesh.shape["seq"], mesh.shape["head"])

    def on_device(tokens, norm_gain, w_up, w_down, routes, combine, loss_mask):
        rows, width = tokens.shape
        peers = sizes[1] * sizes[2]
        slots = peers * CAP
        folded = (4, slots * FOLD, width // FOLD)
        vmem = pl.BlockSpec(memory_space=pltpu.VMEM)
        hbm = pl.BlockSpec(memory_space=pltpu.HBM)
        keep = lambda x: pltpu.with_memory_space_constraint(x, pltpu.HBM)
        grad_tokens, grad_gain, grad_combine, loss = pl.pallas_call(
            lambda *refs: kernel(sizes, *refs),
            out_shape=(
                jax.ShapeDtypeStruct((rows, width), BF16),
                jax.ShapeDtypeStruct((width // 128, 128), F32),
                jax.ShapeDtypeStruct((2, rows), F32),
                jax.ShapeDtypeStruct((1, 1), F32),
            ),
            in_specs=[hbm] * 7,
            out_specs=(vmem, vmem, vmem, vmem),
            scratch_shapes=[
                pltpu.VMEM((rows, width), BF16),
                pltpu.VMEM((width // 128, 128), F32),
                pltpu.VMEM((2, rows), I32),
                pltpu.VMEM((2, rows), F32),
                pltpu.VMEM((1, rows), I32),
                pltpu.VMEM((1, width), F32),
                pltpu.VMEM((rows, 1), F32),
                pltpu.VMEM(w_up.shape[1:], BF16),
                pltpu.VMEM(w_down.shape[1:], BF16),
                pltpu.VMEM(w_up.shape[1:], BF16),
                pltpu.VMEM(w_down.shape[1:], BF16),
                pltpu.VMEM(folded, BF16),
                pltpu.VMEM(folded, BF16),
                pltpu.VMEM((slots, width), BF16),
                pltpu.VMEM((slots, width), F32),
                pltpu.VMEM((slots, width), BF16),
                pltpu.VMEM((2 * rows, slots), BF16),
                pltpu.VMEM((rows, width), F32),
                pltpu.VMEM((16, 128), F32),
                pltpu.VMEM((sizes[0] + 1, 16, 128), F32),
                pltpu.VMEM((sizes[1] + 1, 16, 128), F32),
                pltpu.VMEM((sizes[2] + 1, 16, 128), F32),
                pltpu.VMEM((8, 128), F32),
                pltpu.VMEM((sizes[0] + 1, 8, 128), F32),
                pltpu.VMEM((sizes[1] + 1, 8, 128), F32),
                pltpu.VMEM((sizes[2] + 1, 8, 128), F32),
                pltpu.VMEM((16, 128), F32),
                pltpu.VMEM((8, 128), F32),
                pltpu.SemaphoreType.DMA((4,)),
                pltpu.SemaphoreType.DMA((4, CHUNKS)),
                pltpu.SemaphoreType.DMA((8,)),
                pltpu.SemaphoreType.DMA((6,)),
                pltpu.SemaphoreType.DMA((6,)),
                pltpu.SemaphoreType.REGULAR,
                pltpu.SemaphoreType.DMA((2,)),
                pltpu.SemaphoreType.DMA((2,)),
            ],
            compiler_params=pltpu.CompilerParams(
                collective_id=1, has_side_effects=True, vmem_limit_bytes=48 * 2**20),
            cost_estimate=pl.CostEstimate(
                flops=8 * slots * width * width, bytes_accessed=4 * width * width,
                transcendentals=slots * width),
            name="moe",
        )(*map(keep, (tokens, norm_gain.reshape(width // 128, 128), w_up, w_down, routes.T,
                      combine.T, loss_mask.reshape(1, rows))))
        return grad_tokens, grad_gain.reshape(width), grad_combine.T, loss.reshape(())

    split = ("dp", "seq", "head")
    in_specs = (P(split, None), P(), P(("seq", "head"), None, None), P(("seq", "head"), None, None),
                P(split, None), P(split, None), P(split))
    out_specs = (P(split, None), P(), P(split, None), P())
    return jax.shard_map(on_device, mesh=mesh, in_specs=in_specs, out_specs=out_specs,
                         check_vma=False)
```
